32 devices in a mesh: ctx: 8 (over y, x, core), head: 4 (over z).
Axes of the slice: x: 2, y: 2, z: 4, core: 2. Of those that a mesh axis runs over, the one named last changes fastest.
Arguments:
- queries: bfloat16 [4096, 4096], P('ctx', 'head'), may hold values from -0.59765625 to 0.59765625
- keys: bfloat16 [4096, 4096], P('ctx', 'head'), may hold values from -0.59765625 to 0.59765625
- values: bfloat16 [4096, 4096], P('ctx', 'head'), may hold values from -6 to 6
- gates: float32 [32, 7, 4096], P('head', None, 'ctx'), may hold values from 0.05 to 1
- segment_ids: int32 [4096], P('ctx'), may hold values from 0 to 2, never falling along the last dimension, each value on 1 to 3072 neighbouring positions
- out_weight: bfloat16 [4096, 4096], P('head'), may hold values from -0.09375 to 0.09375
- out_grad: bfloat16 [4096, 4096], P('ctx', 'head'), may hold values from -0.59765625 to 0.59765625
Outputs:
- mixed: bfloat16 [4096, 4096], P('ctx', 'head')
- grad_queries: bfloat16 [4096, 4096], P('ctx', 'head')
- grad_keys: bfloat16 [4096, 4096], P('ctx', 'head')
- grad_values: bfloat16 [4096, 4096], P('ctx', 'head')
The draws below stay inside these ranges and needn't reach their ends.
Inputs may be any that keep to these rules, and one draw needn't show every extreme that they name: `segment_ids`: segment ids never fall along the sequence: each document is one run of consecutive tokens; one document has exactly 3072 tokens.
All inputs are finite; a program needn't handle non-finite values.
Results may differ from the reference program's by a relative error of at most 0.018.
Values may be sent and summed in bfloat16 or wider, within the bound.
A program may use at most 64 MiB of HBM per device.

```python
import math
import jax
import jax.numpy as jnp
import numpy as np
from jax import lax

D = 4096
HEADS = 32
DK = 128
DV = 128
SPAN = 64
DOCS = 3
TOK_DEV = 512
TOKENS = 4096
NEAR_LEVELS = 4
LEVELS = 7
N_CTX = 8
N_HEAD = 4


def shard_levels(stream_key, extent, shards, least, top_value):
    factor_of, own = 1.0, jax.random.fold_in(stream_key, 6)
    for axis_at, parts in shards:
        steps = jnp.exp(jax.random.uniform(jax.random.fold_in(own, axis_at), (parts,), jnp.float32, least / len(shards), top_value / len(shards)))
        factor_of = factor_of * jnp.repeat(steps, extent[axis_at] // parts).reshape([-1 if axis == axis_at else 1 for axis in range(len(extent))])
    return factor_of


def profile(number_of, total, reach, skew):
    weights = [(1 << 20) // math.isqrt(rank ** skew) + 1 for rank in range(2, number_of + 1)]
    spare, holding = total - reach - (number_of - 1), [1] * (number_of - 1)
    while spare > 0:
        movable = [i for i in range(number_of - 1) if holding[i] < reach]
        pool, left = sum([weights[i] for i in movable]), spare
        for i in movable:
            more = min(reach - holding[i], max(1, left * weights[i] // pool), spare)
            holding[i] = holding[i] + more
            spare = spare - more
    return np.array([reach] + holding)


def ragged(key, amount, total, limit, lean):
    if amount == 2:
        one = jax.random.randint(key, (), max(1, total - limit), min(limit, total - 1) + 1)
        return jnp.stack([one, total - one])
    sizes = jnp.asarray(profile(amount, total, limit, lean), jnp.int32)
    couples = (amount - 1) // 2
    giver, taker = sizes[1:1 + 2 * couples:2], sizes[2:2 + 2 * couples:2]
    room = jnp.minimum(giver - 1, limit - taker)
    passed = jax.random.randint(jax.random.fold_in(key, 1), (couples,), 0, 1 << 20) % (room + 1)
    sizes = sizes.at[1:1 + 2 * couples:2].set(giver - passed).at[2:2 + 2 * couples:2].set(taker + passed)
    return sizes[jax.random.permutation(jax.random.fold_in(key, 2), amount)]


def scatter_about(own_key, dims, scale, limit, pieces=(), held_as=jnp.bfloat16):
    level = shard_levels(own_key, dims, pieces, -0.22, 0.18) if pieces else 1.0
    values = jax.random.normal(own_key, dims, jnp.float32) * scale * level
    return jnp.minimum(jnp.maximum(values, -limit), limit).astype(held_as)


def setup_inputs(seed: int = 0) -> dict:
    arg_keys = jax.random.split(jax.random.key(seed), 8)
    queries = scatter_about(arg_keys[0], (TOKENS, HEADS * DK), 0.1, 0.59765625, ((0, 8), (1, 4)))
    keys = scatter_about(arg_keys[1], (TOKENS, HEADS * DK), 0.1, 0.59765625, ((0, 8), (1, 4)))
    values = scatter_about(arg_keys[2], (TOKENS, HEADS * DV), 1.0, 6.0, ((0, 8), (1, 4)))
    gates = jnp.clip(jnp.exp(math.log(1.0) - 2.9957323 * jax.random.uniform(arg_keys[3], (HEADS, LEVELS, TOKENS), jnp.float32) ** shard_levels(arg_keys[3], (HEADS, LEVELS, TOKENS), ((0, 4), (2, 8)), -0.2, 0.2)), 0.05, 1.0)
    segment_ids = jnp.searchsorted(jnp.cumsum(ragged(arg_keys[4], DOCS, TOKENS, TOKENS * 3 // 4, 0)), jnp.arange(TOKENS), side="right").astype(jnp.int32)
    out_weight = scatter_about(arg_keys[5], (HEADS * DV, D), (HEADS * DV) ** -0.5, 0.09375, ((0, 4),))
    out_grad = scatter_about(arg_keys[6], (TOKENS, D), 0.1, 0.59765625, ((0, 8), (1, 4)))
    return {"queries": queries, "keys": keys, "values": values, "gates": gates, "segment_ids": segment_ids, "out_weight": out_weight, "out_grad": out_grad}


highest = lax.Precision.HIGHEST


def level_table(count):
    span_ids = jnp.arange(count, dtype=jnp.int32) // SPAN
    differ = jnp.bitwise_xor(span_ids[:, None], span_ids[None, :])
    levels = jnp.zeros((count, count), jnp.int32)
    for section in range(NEAR_LEVELS - 1):
        levels = levels + (differ >= (1 << section)).astype(jnp.int32)
    return levels


def near_block(block, levels):
    query, key, value, grad_out, gate, segment = block
    count = query.shape[0]
    positions = jnp.arange(count, dtype=jnp.int32)
    allowed = (positions[:, None] >= positions[None, :]) & (segment[:, None] == segment[None, :])
    weight = jnp.zeros((count, count), jnp.float32)
    for level_id in range(NEAR_LEVELS):
        weight = weight + jnp.where(levels == level_id, gate[level_id][:, None], jnp.float32(0))
    weight = jnp.where(allowed, weight, jnp.float32(0))
    scores = jnp.dot(query, key.T, preferred_element_type=jnp.float32)
    near_probs = (weight * scores).astype(jnp.bfloat16)
    result = jnp.dot(near_probs, value, preferred_element_type=jnp.float32)
    value_scores = jnp.dot(grad_out, value.T, preferred_element_type=jnp.float32)
    grad_scores = (weight * value_scores).astype(jnp.bfloat16)
    grad_query = jnp.dot(grad_scores, key, preferred_element_type=jnp.float32)
    grad_key = jnp.dot(grad_scores.T, query, preferred_element_type=jnp.float32)
    grad_value = jnp.dot(near_probs.T, grad_out, preferred_element_type=jnp.float32)
    return result, grad_query, grad_key, grad_value


def reference(queries, keys, values, gates, segment_ids, out_weight, out_grad):
    grad_attention = jnp.dot(out_grad, out_weight.T, preferred_element_type=jnp.float32).astype(jnp.bfloat16)
    levels = level_table(TOK_DEV)

    def split_heads(array, width):
        return array.reshape(TOKENS, HEADS, width).transpose(1, 0, 2)

    def near_one(block):
        return near_block(block, levels)

    def head_terms(items):
        query, key, value, grad_out, gate = items
        blocks = (query.reshape(N_CTX, TOK_DEV, DK), key.reshape(N_CTX, TOK_DEV, DK),
                  value.reshape(N_CTX, TOK_DEV, DV), grad_out.reshape(N_CTX, TOK_DEV, DV),
                  gate.reshape(LEVELS, N_CTX, TOK_DEV).transpose(1, 0, 2),
                  segment_ids.reshape(N_CTX, TOK_DEV))
        near = jax.vmap(near_one)(blocks)
        result = near[0].reshape(TOKENS, DV)
        grad_query = near[1].reshape(TOKENS, DK)
        grad_key = near[2].reshape(TOKENS, DK)
        grad_value = near[3].reshape(TOKENS, DV)
        query_wide = query.astype(jnp.float32)
        key_wide = key.astype(jnp.float32)
        value_wide = value.astype(jnp.float32)
        grad_wide = grad_out.astype(jnp.float32)
        for level_id in range(NEAR_LEVELS, LEVELS):
            run = SPAN * 2 ** (level_id - 1)
            groups = TOKENS // (2 * run)
            query_runs = query_wide.reshape(groups, 2, run, DK)
            key_runs = key_wide.reshape(groups, 2, run, DK)
            value_runs = value_wide.reshape(groups, 2, run, DV)
            grad_runs = grad_wide.reshape(groups, 2, run, DV)
            segment_runs = segment_ids.reshape(groups, 2, run)
            end_seg = segment_runs[:, 0, run - 1]
            low_keep = (segment_runs[:, 0, :] == end_seg[:, None]).astype(jnp.float32)
            high_keep = (segment_runs[:, 1, :] == end_seg[:, None]).astype(jnp.float32)
            high_gate = gate[level_id].reshape(groups, 2, run)[:, 1, :] * high_keep
            state = jnp.einsum("gsd,gse->gde", key_runs[:, 0] * low_keep[..., None], value_runs[:, 0], precision=highest)
            dual = jnp.einsum("gtd,gte->gde", query_runs[:, 1] * high_gate[..., None], grad_runs[:, 1], precision=highest)
            high_out = jnp.einsum("gtd,gde->gte", query_runs[:, 1], state, precision=highest) * high_gate[..., None]
            high_dq = jnp.einsum("gte,gde->gtd", grad_runs[:, 1], state, precision=highest) * high_gate[..., None]
            low_dk = jnp.einsum("gse,gde->gsd", value_runs[:, 0], dual, precision=highest) * low_keep[..., None]
            low_dv = jnp.einsum("gsd,gde->gse", key_runs[:, 0], dual, precision=highest) * low_keep[..., None]
            result = result + jnp.stack([jnp.zeros_like(high_out), high_out], 1).reshape(TOKENS, DV)
            grad_query = grad_query + jnp.stack([jnp.zeros_like(high_dq), high_dq], 1).reshape(TOKENS, DK)
            grad_key = grad_key + jnp.stack([low_dk, jnp.zeros_like(low_dk)], 1).reshape(TOKENS, DK)
            grad_value = grad_value + jnp.stack([low_dv, jnp.zeros_like(low_dv)], 1).reshape(TOKENS, DV)
        return result, grad_query, grad_key, grad_value

    terms = lax.map(head_terms, (split_heads(queries, DK), split_heads(keys, DK), split_heads(values, DV),
                                 split_heads(grad_attention, DV), gates))
    attention = terms[0].transpose(1, 0, 2).reshape(TOKENS, HEADS * DV).astype(jnp.bfloat16)
    group = HEADS * DV // N_HEAD
    mixed = jnp.zeros((TOKENS, D), jnp.float32)
    for part_id in range(N_HEAD):
        term = jnp.dot(attention[:, part_id * group:(part_id + 1) * group],
                       out_weight[part_id * group:(part_id + 1) * group], preferred_element_type=jnp.float32)
        rounded = lax.optimization_barrier(term.astype(jnp.bfloat16))
        mixed = mixed + rounded.astype(jnp.float32)
    grad_queries = terms[1].transpose(1, 0, 2).reshape(TOKENS, HEADS * DK).astype(jnp.bfloat16)
    grad_keys = terms[2].transpose(1, 0, 2).reshape(TOKENS, HEADS * DK).astype(jnp.bfloat16)
    grad_values = terms[3].transpose(1, 0, 2).reshape(TOKENS, HEADS * DV).astype(jnp.bfloat16)
    return (mixed.astype(jnp.bfloat16), grad_queries, grad_keys, grad_values)
```

```python
import functools

import jax
import jax.numpy as jnp
from jax import lax
from jax.experimental import pallas as pl
from jax.experimental.pallas import tpu as pltpu
from jax.sharding import PartitionSpec as P

SPAN = 64
F32 = jnp.float32
BF16 = jnp.bfloat16


def mm(a, b, ca=1, cb=0):
    return lax.dot_general(a, b, (((ca,), (cb,)), ((), ())), preferred_element_type=F32)


def table(seg_col, seg_row, rows, near):
    t = lax.broadcasted_iota(jnp.int32, (rows, rows), 0)
    s = lax.broadcasted_iota(jnp.int32, (rows, rows), 1)
    differ = jnp.bitwise_xor(t // SPAN, s // SPAN)
    level = jnp.zeros((rows, rows), jnp.int32)
    for section in range(near - 1):
        level = level + (differ >= 1 << section).astype(jnp.int32)
    return jnp.where((t >= s) & (seg_col == seg_row), level, near)


def near_weight(table_ref, cols, near):
    level = table_ref[...]
    weight = jnp.zeros(level.shape, F32)
    for j in range(near):
        weight = jnp.where(level == j, cols[:, j : j + 1], weight)
    return weight


def summary_kernel(levels, k_ref, v_ref, ext_ref, out_ref):
    cols = ext_ref[0].T
    seg = cols[:, levels : levels + 1]
    keep = (seg == seg[-1:, :]).astype(F32)
    masked = (k_ref[...].astype(F32) * keep).astype(BF16)
    out_ref[0] = mm(masked, v_ref[...], 0, 0).astype(BF16)


def forward_kernel(near, levels, q_ref, k_ref, v_ref, ext_ref, inc_ref, out_ref, table_ref):
    rows = q_ref.shape[0]
    ext = ext_ref[0]
    cols = ext.T

    @pl.when(pl.program_id(0) == 0)
    def _():
        table_ref[...] = table(cols[:, levels : levels + 1], ext[levels : levels + 1], rows, near)

    q = q_ref[...]
    weight = near_weight(table_ref, cols, near)
    probs = (weight * mm(q, k_ref[...], 1, 1)).astype(BF16)
    out = mm(probs, v_ref[...])
    for j in range(levels - near):
        out = out + cols[:, near + j : near + j + 1] * mm(q, inc_ref[j, 0])
    out_ref[...] = out.astype(BF16)


def leaf_kernel(near, levels, q_ref, g_ref, ext_ref, out_ref):
    cols = ext_ref[0].T
    q = q_ref[...]
    g = g_ref[...].astype(F32)
    for j in range(levels - near):
        scaled = (g * cols[:, near + j : near + j + 1]).astype(BF16)
        out_ref[j, 0] = mm(q, scaled, 0, 0).astype(BF16)


def backward_kernel(
    near, levels, q_ref, k_ref, v_ref, g_ref, ext_ref, inc_ref, dq_ref, dk_ref, dv_ref, table_ref
):
    rows = q_ref.shape[0]
    ext = ext_ref[0]
    cols = ext.T

    @pl.when(pl.program_id(0) == 0)
    def _():
        table_ref[...] = table(cols[:, levels : levels + 1], ext[levels : levels + 1], rows, near)

    q, k, v, g = q_ref[...], k_ref[...], v_ref[...], g_ref[...]
    weight = near_weight(table_ref, cols, near)
    probs = (weight * mm(q, k, 1, 1)).astype(BF16)
    dv_ref[...] = mm(probs, g, 0, 0)
    grads = (weight * mm(g, v, 1, 1)).astype(BF16)
    dk_ref[...] = mm(grads, q, 0, 0)
    dq = mm(grads, k)
    for j in range(levels - near):
        dq = dq + cols[:, near + j : near + j + 1] * mm(g, inc_ref[j, 0], 1, 1)
    dq_ref[...] = dq.astype(BF16)


def finish_kernel(levels, k_ref, v_ref, ext_ref, in_ref, ndk_ref, ndv_ref, dk_ref, dv_ref):
    seg = ext_ref[0].T[:, levels : levels + 1]
    keep = (seg == seg[-1:, :]).astype(F32)
    state = in_ref[0]
    dk_ref[...] = (ndk_ref[...] + keep * mm(v_ref[...], state, 1, 1)).astype(BF16)
    dv_ref[...] = (ndv_ref[...] + keep * mm(k_ref[...], state)).astype(BF16)


def head_call(kernel, heads, args, specs, outs, out_specs, flops, scratch=()):
    return pl.pallas_call(
        kernel,
        grid=(heads,),
        in_specs=specs,
        out_specs=out_specs,
        out_shape=outs,
        scratch_shapes=scratch,
        cost_estimate=pl.CostEstimate(flops=flops, bytes_accessed=1 << 22, transcendentals=0),
        compiler_params=pltpu.CompilerParams(vmem_limit_bytes=40 << 20),
    )(*args)


def swap(value, axis, section):
    pairs = [(i, i ^ (1 << section)) for i in range(lax.axis_size(axis))]
    return lax.ppermute(value, axis, pairs)


def shards(queries, keys, values, gates, segment_ids, out_weight, out_grad):
    rows = queries.shape[0]
    heads, levels = gates.shape[0], gates.shape[1]
    dk = queries.shape[1] // heads
    dv = values.shape[1] // heads
    near = (rows // SPAN).bit_length()
    spread = lax.axis_size("ctx").bit_length() - 1
    me = lax.axis_index("ctx")
    z = lax.axis_index("head")
    count = lax.axis_size("head")
    width = out_grad.shape[1]

    ends = jnp.stack([segment_ids[0], segment_ids[rows - 1]]).astype(F32)
    marks = lax.all_gather(ends, "ctx")
    first, last = ends[0], ends[1]

    seg = segment_ids.astype(F32)
    keep_high = (segment_ids == segment_ids[0]).astype(F32)
    size = -(-(levels + 1) // 8) * 8
    ext = jnp.concatenate(
        [
            gates[:, :near],
            gates[:, near:] * keep_high,
            jnp.broadcast_to(seg, (heads, 1, rows)),
            jnp.zeros((heads, size - levels - 1, rows), F32),
        ],
        axis=1,
    )

    kspec = pl.BlockSpec((rows, dk), lambda h: (0, h))
    vspec = pl.BlockSpec((rows, dv), lambda h: (0, h))
    espec = pl.BlockSpec((1, size, rows), lambda h: (h, 0, 0))
    sspec = pl.BlockSpec((1, dk, dv), lambda h: (h, 0, 0))
    ispec = pl.BlockSpec((levels - near, 1, dk, dv), lambda h: (0, h, 0, 0))
    wide = jax.ShapeDtypeStruct((rows, heads * dk), BF16)
    wide_v = jax.ShapeDtypeStruct((rows, heads * dv), BF16)
    scratch = [pltpu.VMEM((rows, rows), jnp.int32)]
    near_flops = 2 * rows * rows * dk * heads

    def product(block, owner):
        part = lax.dynamic_slice_in_dim(out_weight, owner * width, width, 1)
        return mm(block, part, 1, 1)

    going_right = going_left = out_grad
    received = []
    for step in range(count - 1):
        going_right = lax.ppermute(
            going_right, "head", [(i, i + 1) for i in range(step, count - 1)]
        )
        going_left = lax.ppermute(going_left, "head", [(i, i - 1) for i in range(1, count - step)])
        received.append((going_right, going_left))
    total = product(out_grad, z)

    state = head_call(
        functools.partial(summary_kernel, levels),
        heads,
        (keys, values, ext),
        [kspec, vspec, espec],
        jax.ShapeDtypeStruct((heads, dk, dv), BF16),
        sspec,
        2 * rows * dk * dv * heads,
    )
    pieces = []
    for section in range(spread):
        low = (1 << section) - 1
        partner = swap(state, "ctx", section)
        upper = (me >> section) & 1 == 1
        partner_mark = marks[(me ^ (1 << section)) | low, 1]
        own_mark = marks[me | low, 1]
        zero = jnp.zeros((), BF16)
        pieces.append(jnp.where(upper & (partner_mark == first), partner, zero))
        joined = partner_mark == own_mark
        state = jnp.where(upper | joined, state, zero) + jnp.where(upper & ~joined, zero, partner)
    incoming = jnp.stack(pieces)
    attention = head_call(
        functools.partial(forward_kernel, near, levels),
        heads,
        (queries, keys, values, ext, incoming),
        [kspec, kspec, vspec, espec, ispec],
        wide_v,
        vspec,
        3 * near_flops,
        scratch,
    )

    projected = mm(attention, out_weight).astype(BF16)

    def share(owner):
        return lax.dynamic_slice_in_dim(projected, owner * width, width, 1).astype(F32)

    sum_right = sum_left = None
    for step in range(count - 1):
        reach = count - 1 - step
        mine_right = share(jnp.minimum(z + reach, count - 1))
        mine_left = share(jnp.maximum(z - reach, 0))
        if step:
            mine_right = mine_right + sum_right.astype(F32)
            mine_left = mine_left + sum_left.astype(F32)
        sum_right = lax.ppermute(
            mine_right.astype(BF16), "head", [(i, i + 1) for i in range(step + 1)]
        )
        sum_left = lax.ppermute(
            mine_left.astype(BF16), "head", [(i, i - 1) for i in range(reach, count)]
        )
    mixed = (share(z) + sum_right.astype(F32) + sum_left.astype(F32)).astype(BF16)

    for step, (right, left) in enumerate(received):
        if step == count - 2:
            end = z == count - 1
            total = total + product(
                jnp.where(end, right, left), jnp.where(end, 0, count - 1)
            )
        else:
            total = total + product(right, jnp.maximum(z - step - 1, 0))
            total = total + product(left, jnp.minimum(z + step + 1, count - 1))
    cot = total.astype(BF16)

    dual = head_call(
        functools.partial(leaf_kernel, near, levels),
        heads,
        (queries, cot, ext),
        [kspec, vspec, espec],
        jax.ShapeDtypeStruct((levels - near, heads, dk, dv), BF16),
        ispec,
        2 * rows * dk * dv * heads * (levels - near),
    )
    inbound = jnp.zeros((heads, dk, dv), F32)
    for section in range(spread):
        low = (1 << section) - 1
        partner = swap(dual, "ctx", section)
        upper = (me >> section) & 1 == 1
        partner_mark = marks[(me ^ (1 << section)) & ~low, 0]
        own_mark = marks[me & ~low, 0]
        zero = jnp.zeros((), BF16)
        inbound = inbound + jnp.where(~upper & (partner_mark == last), partner[0], zero).astype(F32)
        joined = partner_mark == own_mark
        dual = jnp.where(upper & ~joined, zero, dual[1:]) + jnp.where(
            upper | joined, partner[1:], zero
        )
    near_dk = jax.ShapeDtypeStruct((rows, heads * dk), F32)
    near_dv = jax.ShapeDtypeStruct((rows, heads * dv), F32)
    grad_queries, near_dk, near_dv = head_call(
        functools.partial(backward_kernel, near, levels),
        heads,
        (queries, keys, values, cot, ext, incoming),
        [kspec, kspec, vspec, vspec, espec, ispec],
        (wide, near_dk, near_dv),
        (kspec, kspec, vspec),
        6 * near_flops,
        scratch,
    )
    grad_keys, grad_values = head_call(
        functools.partial(finish_kernel, levels),
        heads,
        (keys, values, ext, inbound.astype(BF16), near_dk, near_dv),
        [kspec, vspec, espec, sspec, kspec, vspec],
        (wide, wide_v),
        (kspec, vspec),
        4 * rows * dk * dv * heads,
    )
    return (mixed, grad_queries, grad_keys, grad_values)


def solution(mesh):
    placed = (
        P("ctx", "head"),
        P("ctx", "head"),
        P("ctx", "head"),
        P("head", None, "ctx"),
        P("ctx"),
        P("head", None),
        P("ctx", "head"),
    )
    return jax.shard_map(
        shards,
        mesh=mesh,
        in_specs=placed,
        out_specs=(P("ctx", "head"), P("ctx", "head"), P("ctx", "head"), P("ctx", "head")),
        check_vma=False,
    )
```

```python
import functools

import jax
import jax.numpy as jnp
from jax import lax
from jax.experimental import pallas as pl
from jax.experimental.pallas import tpu as pltpu
from jax.sharding import PartitionSpec as P

SPAN = 64
F32 = jnp.float32
BF16 = jnp.bfloat16
MESH = pl.DeviceIdType.MESH


def mm(a, b, ca=1, cb=0):
    return lax.dot_general(a, b, (((ca,), (cb,)), ((), ())), preferred_element_type=F32)


def table(seg_col, seg_row, rows, near):
    t = lax.broadcasted_iota(jnp.int32, (rows, rows), 0)
    s = lax.broadcasted_iota(jnp.int32, (rows, rows), 1)
    differ = jnp.bitwise_xor(t // SPAN, s // SPAN)
    level = jnp.zeros((rows, rows), jnp.int32)
    for section in range(near - 1):
        level = level + (differ >= 1 << section).astype(jnp.int32)
    return jnp.where((t >= s) & (seg_col == seg_row), level, near)


def kernel(
    n_ctx,
    n_head,
    heads,
    levels,
    near,
    q_ref,
    k_ref,
    v_ref,
    og_ref,
    ext_ref,
    w_hbm,
    mixed_ref,
    dq_ref,
    dk_ref,
    dv_ref,
    w_ref,
    gath,
    acc,
    near_out,
    pj,
    rsr,
    rsl,
    weights,
    probs,
    table_ref,
    cols_ref,
    cot,
    state_out,
    state_in,
    marks_out,
    marks_in,
    pieces,
    dual_out,
    dual_in,
    inbound,
    w_sem,
    ag_recv,
    ag_right,
    ag_left,
    rs_recv_r,
    rs_recv_l,
    rs_right,
    rs_left,
    st_send,
    st_recv,
    mk_send,
    mk_recv,
    du_send,
    du_recv,
):
    rows = q_ref.shape[0]
    dk = q_ref.shape[1] // heads
    dv = v_ref.shape[1] // heads
    width = og_ref.shape[1]
    inner = w_ref.shape[0]
    far = levels - near
    spread = n_ctx.bit_length() - 1
    me = lax.axis_index("ctx")
    z = lax.axis_index("head")
    not_first = z > 0
    not_last = z < n_head - 1
    bits = [(me // (1 << s)) % 2 for s in range(spread)]
    partners = [me + (1 - 2 * bits[s]) * (1 << s) for s in range(spread)]

    def remote(src, dst, send, recv, device):
        return pltpu.make_async_remote_copy(
            src_ref=src,
            dst_ref=dst,
            send_sem=send,
            recv_sem=recv,
            device_id=device,
            device_id_type=MESH,
        )

    load = pltpu.make_async_copy(w_hbm, w_ref, w_sem)
    load.start()

    barrier = pltpu.get_barrier_semaphore()
    for s in range(spread):
        pl.semaphore_signal(barrier, inc=1, device_id=(partners[s], z), device_id_type=MESH)

    @pl.when(not_first)
    def _():
        pl.semaphore_signal(barrier, inc=1, device_id=(me, z - 1), device_id_type=MESH)

    @pl.when(not_last)
    def _():
        pl.semaphore_signal(barrier, inc=1, device_id=(me, z + 1), device_id_type=MESH)

    pl.semaphore_wait(
        barrier, spread + not_first.astype(jnp.int32) + not_last.astype(jnp.int32)
    )

    def own_right():
        return remote(og_ref, gath.at[z], ag_right.at[z], ag_recv.at[z], (me, z + 1))

    def own_left():
        return remote(og_ref, gath.at[z], ag_left.at[z], ag_recv.at[z], (me, z - 1))

    def pass_right(owner):
        return remote(
            gath.at[owner], gath.at[owner], ag_right.at[owner], ag_recv.at[owner], (me, z + 1)
        )

    def pass_left(owner):
        return remote(
            gath.at[owner], gath.at[owner], ag_left.at[owner], ag_recv.at[owner], (me, z - 1)
        )

    @pl.when(not_last)
    def _():
        own_right().start()

    @pl.when(not_first)
    def _():
        own_left().start()

    def head_k(h):
        return pl.ds(pl.multiple_of(h * dk, dk), dk)

    def head_v(h):
        return pl.ds(pl.multiple_of(h * dv, dv), dv)

    @pl.loop(0, heads)
    def _(h):
        cols = ext_ref[h].T
        cols_ref[h] = cols
        seg = cols[:, levels : levels + 1]
        keep = (seg == seg[rows - 1 : rows, :]).astype(F32)
        masked = (k_ref[:, head_k(h)].astype(F32) * keep).astype(BF16)
        state_out[0, h] = mm(masked, v_ref[:, head_v(h)], 0, 0).astype(BF16)

    seg_row = ext_ref[0, levels : levels + 1, :]
    lane = dv
    first = jnp.broadcast_to(seg_row[:, 0:1], (1, lane))
    last = jnp.broadcast_to(seg_row[:, rows - 1 : rows], (1, lane))
    marks_out[0, 0:8, :] = jnp.broadcast_to(first, (8, lane))
    marks_out[0, 8:16, :] = jnp.broadcast_to(last, (8, lane))

    def hop(s):
        return (
            remote(
                state_out.at[s], state_in.at[s], st_send.at[s], st_recv.at[s], (partners[s], z)
            ),
            remote(
                marks_out.at[s], marks_in.at[s], mk_send.at[s], mk_recv.at[s], (partners[s], z)
            ),
        )

    def hop_start(s):
        for copy in hop(s):
            copy.start()

    def hop_finish(s):
        for copy in hop(s):
            copy.wait_recv()
        up = bits[s].astype(F32)
        own_first, own_last = marks_out[s, 0:1, :], marks_out[s, 8:9, :]
        its_first, its_last = marks_in[s, 0:1, :], marks_in[s, 8:9, :]
        joined = (its_last == own_last).astype(F32)
        linked = (its_last == first).astype(F32) * up
        mine = up + (1 - up) * joined
        theirs = (1 - up) + up * joined
        last_section = s == spread - 1

        @pl.loop(0, heads)
        def _(h):
            partner = state_in[s, h].astype(F32)
            pieces[s, h] = (partner * linked).astype(BF16)
            if not last_section:
                state_out[s + 1, h] = (
                    state_out[s, h].astype(F32) * mine + partner * theirs
                ).astype(BF16)

        if not last_section:
            marks_out[s + 1, 0:8, :] = jnp.broadcast_to(
                up * its_first + (1 - up) * own_first, (8, lane)
            )
            marks_out[s + 1, 8:16, :] = jnp.broadcast_to(
                up * own_last + (1 - up) * its_last, (8, lane)
            )
            hop_start(s + 1)

    if spread:
        hop_start(0)

    table_ref[...] = table(
        cols_ref[0][:, levels : levels + 1], ext_ref[0, levels : levels + 1, :], rows, near
    )
    tile = 256

    def near_forward(low, high):
        @pl.loop(low, high)
        def _(h):
            cols = cols_ref[h]
            level = table_ref[...]
            weight = jnp.zeros((rows, rows), F32)
            for j in range(near):
                weight = jnp.where(level == j, cols[:, j : j + 1], weight)
            weights[h] = weight.astype(BF16)
            p = (weight * mm(q_ref[:, head_k(h)], k_ref[:, head_k(h)], 1, 1)).astype(BF16)
            probs[h] = p
            near_out[:, head_v(h)] = mm(p, v_ref[:, head_v(h)])

    done = 0
    for s in range(spread):
        upto = heads * (s + 1) // spread
        near_forward(done, upto)
        done = upto
        hop_finish(s)
    if done < heads:
        near_forward(done, heads)

    def far_gates(h):
        cols = cols_ref[h]
        seg = cols[:, levels : levels + 1]
        keep = (seg == seg[0:1, :]).astype(F32)
        return [cols[:, near + j : near + j + 1] * keep for j in range(far)]

    @pl.loop(0, heads)
    def _(h):
        gates = far_gates(h)
        q = q_ref[:, head_k(h)]
        out = near_out[:, head_v(h)]
        for j in range(far):
            out = out + gates[j] * mm(q, pieces[j, h])
        mixed_ref[:, head_v(h)] = out.astype(BF16)

    load.wait()

    flip = (z < n_head - z).astype(jnp.int32)
    for at in range(n_head):
        dest = flip * (n_head - 1 - at) + (1 - flip) * at

        @pl.loop(0, width // tile)
        def _(c):
            from_col = pl.multiple_of(dest * width + c * tile, tile)
            part = mm(mixed_ref[...], w_ref[:, pl.ds(from_col, tile)])
            pj[dest, :, pl.ds(pl.multiple_of(c * tile, tile), tile)] = part.astype(BF16)

    def product(block, owner, fresh):
        @pl.loop(0, inner // tile)
        def _(r):
            at = pl.ds(pl.multiple_of(r * tile, tile), tile)
            part = mm(
                block[...], w_ref[at, pl.ds(pl.multiple_of(owner * width, width), width)], 1, 1
            )
            acc[:, at] = part if fresh else acc[:, at] + part

    product(og_ref, z, True)

    def sum_right(dest, src=rsr):
        return remote(src.at[dest], rsr.at[dest], rs_right.at[dest], rs_recv_r.at[dest], (me, z + 1))

    def sum_left(dest, src=rsl):
        return remote(src.at[dest], rsl.at[dest], rs_left.at[dest], rs_recv_l.at[dest], (me, z - 1))

    def add_rows(buf, dest):
        @pl.loop(0, rows // 64)
        def _(r):
            at = pl.ds(pl.multiple_of(r * 64, 64), 64)
            buf[dest, at, :] = (buf[dest, at, :].astype(F32) + pj[dest, at, :].astype(F32)).astype(
                BF16
            )

    def send_sum(buf, make, has_upstream, dest):
        @pl.when(has_upstream)
        def _():
            make(dest).wait_recv()
            add_rows(buf, dest)
            make(dest).start()

        @pl.when(jnp.logical_not(has_upstream))
        def _():
            make(dest, pj).start()

    for phase in range(1, n_head):
        reach = n_head - phase
        from_left, from_right = z - phase, z + phase
        has_left, has_right = from_left >= 0, from_right < n_head

        @pl.when(has_left)
        def _():
            pass_right(from_left).wait_recv()

            @pl.when(not_last)
            def _():
                pass_right(from_left).start()

        @pl.when(has_right)
        def _():
            pass_left(from_right).wait_recv()

            @pl.when(not_first)
            def _():
                pass_left(from_right).start()

        @pl.when(z + reach < n_head)
        def _():
            send_sum(rsr, sum_right, not_first, z + reach)

        @pl.when(z - reach >= 0)
        def _():
            send_sum(rsl, sum_left, not_last, z - reach)

        @pl.when(has_left)
        def _():
            product(gath.at[from_left], from_left, False)

        @pl.when(has_right)
        def _():
            product(gath.at[from_right], from_right, False)

    @pl.loop(0, heads)
    def _(h):
        g = acc[:, head_v(h)].astype(BF16)
        cot[:, head_v(h)] = g
        g = g.astype(F32)
        q = q_ref[:, head_k(h)]
        gates = far_gates(h)
        for j in range(far):
            dual_out[j, h] = mm(q, (g * gates[j]).astype(BF16), 0, 0).astype(BF16)

    starts = [sum(spread - i for i in range(s)) for s in range(spread + 1)]

    def dual_hop(s):
        block = pl.ds(starts[s], spread - s)
        return remote(
            dual_out.at[block], dual_in.at[block], du_send.at[s], du_recv.at[s], (partners[s], z)
        )

    def dual_finish(s):
        dual_hop(s).wait_recv()
        up = bits[s].astype(F32)
        own_first, its_first = marks_out[s, 0:1, :], marks_in[s, 0:1, :]
        joined = (its_first == own_first).astype(F32)
        linked = (its_first == last).astype(F32) * (1 - up)
        mine = (1 - up) + up * joined
        theirs = up + (1 - up) * joined

        @pl.loop(0, heads)
        def _(h):
            gain = dual_in[starts[s], h].astype(F32) * linked
            inbound[h] = gain if s == 0 else inbound[h] + gain
            for j in range(1, spread - s):
                dual_out[starts[s + 1] + j - 1, h] = (
                    dual_out[starts[s] + j, h].astype(F32) * mine
                    + dual_in[starts[s] + j, h].astype(F32) * theirs
                ).astype(BF16)

        if s < spread - 1:
            dual_hop(s + 1).start()

    if spread:
        dual_hop(0).start()

    def near_backward(low, high):
        @pl.loop(low, high)
        def _(h):
            q, k = q_ref[:, head_k(h)], k_ref[:, head_k(h)]
            v, g = v_ref[:, head_v(h)], cot[:, head_v(h)]
            near_out[:, head_v(h)] = mm(probs[h], g, 0, 0)
            grads = (weights[h].astype(F32) * mm(g, v, 1, 1)).astype(BF16)
            acc[:, head_k(h)] = mm(grads, q, 0, 0)
            dq = mm(grads, k)
            gates = far_gates(h)
            for j in range(far):
                dq = dq + gates[j] * mm(g, pieces[j, h], 1, 1)
            dq_ref[:, head_k(h)] = dq.astype(BF16)

    done = 0
    for s in range(spread):
        upto = heads * (s + 1) // spread
        near_backward(done, upto)
        done = upto
        dual_finish(s)
    if done < heads:
        near_backward(done, heads)

    @pl.loop(0, heads)
    def _(h):
        seg = cols_ref[h][:, levels : levels + 1]
        keep = (seg == seg[rows - 1 : rows, :]).astype(F32)
        near_dk, near_dv = acc[:, head_k(h)], near_out[:, head_v(h)]
        if spread:
            state = inbound[h].astype(BF16)
            near_dk = near_dk + keep * mm(v_ref[:, head_v(h)], state, 1, 1)
            near_dv = near_dv + keep * mm(k_ref[:, head_k(h)], state)
        dk_ref[:, head_k(h)] = near_dk.astype(BF16)
        dv_ref[:, head_v(h)] = near_dv.astype(BF16)

    acc[...] = pj[z].astype(F32)

    @pl.when(not_first)
    def _():
        sum_right(z).wait_recv()
        acc[...] = acc[...] + rsr[z].astype(F32)

    @pl.when(not_last)
    def _():
        sum_left(z).wait_recv()
        acc[...] = acc[...] + rsl[z].astype(F32)

    mixed_ref[...] = acc[...].astype(BF16)

    @pl.when(not_last)
    def _():
        own_right().wait_send()

    @pl.when(not_first)
    def _():
        own_left().wait_send()

    for phase in range(1, n_head):
        reach = n_head - phase

        @pl.when((z - phase >= 0) & not_last)
        def _():
            pass_right(z - phase).wait_send()

        @pl.when((z + phase < n_head) & not_first)
        def _():
            pass_left(z + phase).wait_send()

        @pl.when(z + reach < n_head)
        def _():
            sum_right(z + reach).wait_send()

        @pl.when(z - reach >= 0)
        def _():
            sum_left(z - reach).wait_send()

    for s in range(spread):
        for copy in hop(s):
            copy.wait_send()
        dual_hop(s).wait_send()


def shards(queries, keys, values, gates, segment_ids, out_weight, out_grad):
    rows = queries.shape[0]
    heads, levels = gates.shape[0], gates.shape[1]
    dk = queries.shape[1] // heads
    dv = values.shape[1] // heads
    near = (rows // SPAN).bit_length()
    n_ctx = lax.axis_size("ctx")
    n_head = lax.axis_size("head")
    spread = n_ctx.bit_length() - 1
    width = out_grad.shape[1]
    inner = out_weight.shape[0]
    size = -(-(levels + 1) // 8) * 8
    ext = jnp.concatenate(
        [
            gates,
            jnp.broadcast_to(segment_ids.astype(F32), (heads, 1, rows)),
            jnp.zeros((heads, size - levels - 1, rows), F32),
        ],
        axis=1,
    )
    duals = max(spread * (spread + 1) // 2, 1)
    hops = max(spread, 1)
    dma = pltpu.SemaphoreType.DMA
    vmem = pl.BlockSpec(memory_space=pltpu.VMEM)
    return pl.pallas_call(
        functools.partial(kernel, n_ctx, n_head, heads, levels, near),
        in_specs=[vmem] * 5 + [pl.BlockSpec(memory_space=pl.ANY)],
        out_specs=[vmem] * 4,
        out_shape=[
            jax.ShapeDtypeStruct((rows, width), BF16),
            jax.ShapeDtypeStruct(queries.shape, BF16),
            jax.ShapeDtypeStruct(keys.shape, BF16),
            jax.ShapeDtypeStruct(values.shape, BF16),
        ],
        scratch_shapes=[
            pltpu.VMEM(out_weight.shape, BF16),
            pltpu.VMEM((n_head, rows, width), BF16),
            pltpu.VMEM((rows, inner), F32),
            pltpu.VMEM((rows, inner), F32),
            pltpu.VMEM((n_head, rows, width), BF16),
            pltpu.VMEM((n_head, rows, width), BF16),
            pltpu.VMEM((n_head, rows, width), BF16),
            pltpu.VMEM((heads, rows, rows), BF16),
            pltpu.VMEM((heads, rows, rows), BF16),
            pltpu.VMEM((rows, rows), jnp.int32),
            pltpu.VMEM((heads, rows, size), F32),
            pltpu.VMEM((rows, inner), BF16),
            pltpu.VMEM((hops, heads, dk, dv), BF16),
            pltpu.VMEM((hops, heads, dk, dv), BF16),
            pltpu.VMEM((hops, 16, dv), F32),
            pltpu.VMEM((hops, 16, dv), F32),
            pltpu.VMEM((hops, heads, dk, dv), BF16),
            pltpu.VMEM((duals, heads, dk, dv), BF16),
            pltpu.VMEM((duals, heads, dk, dv), BF16),
            pltpu.VMEM((heads, dk, dv), F32),
            dma,
            dma((n_head,)),
            dma((n_head,)),
            dma((n_head,)),
            dma((n_head,)),
            dma((n_head,)),
            dma((n_head,)),
            dma((n_head,)),
            dma((hops,)),
            dma((hops,)),
            dma((hops,)),
            dma((hops,)),
            dma((hops,)),
            dma((hops,)),
        ],
        compiler_params=pltpu.CompilerParams(
            collective_id=0, has_side_effects=True, vmem_limit_bytes=60 << 20
        ),
        cost_estimate=pl.CostEstimate(
            flops=4 * rows * n_head * width * inner + 14 * rows * rows * dk * heads,
            bytes_accessed=40 << 20,
            transcendentals=0,
        ),
    )(queries, keys, values, out_grad, ext, out_weight)


def solution(mesh):
    placed = (
        P("ctx", "head"),
        P("ctx", "head"),
        P("ctx", "head"),
        P("head", None, "ctx"),
        P("ctx"),
        P("head", None),
        P("ctx", "head"),
    )

    def body(*args):
        return tuple(shards(*args))

    return jax.shard_map(
        body,
        mesh=mesh,
        in_specs=placed,
        out_specs=(P("ctx", "head"), P("ctx", "head"), P("ctx", "head"), P("ctx", "head")),
        check_vma=False,
    )
```

```python
import functools

import jax
import jax.numpy as jnp
from jax import lax
from jax.experimental import pallas as pl
from jax.experimental.pallas import tpu as pltpu
from jax.sharding import PartitionSpec as P

SPAN = 64
PARTS = 2
F32 = jnp.float32
BF16 = jnp.bfloat16
MESH = pl.DeviceIdType.MESH


def mm(a, b, ca=1, cb=0):
    return lax.dot_general(a, b, (((ca,), (cb,)), ((), ())), preferred_element_type=F32)


def table(seg_col, seg_row, rows, near):
    t = lax.broadcasted_iota(jnp.int32, (rows, rows), 0)
    s = lax.broadcasted_iota(jnp.int32, (rows, rows), 1)
    differ = jnp.bitwise_xor(t // SPAN, s // SPAN)
    level = jnp.zeros((rows, rows), jnp.int32)
    for section in range(near - 1):
        level = level + (differ >= 1 << section).astype(jnp.int32)
    return jnp.where((t >= s) & (seg_col == seg_row), level, near)


def kernel(
    n_ctx,
    n_head,
    heads,
    levels,
    near,
    q_ref,
    k_ref,
    v_ref,
    og_ref,
    ext_ref,
    w_hbm,
    mixed_ref,
    dq_ref,
    dk_ref,
    dv_ref,
    w_ref,
    gath,
    acc,
    near_out,
    pj,
    rsr,
    rsl,
    weights,
    probs,
    table_ref,
    cols_ref,
    cot,
    state_out,
    state_in,
    marks_out,
    marks_in,
    pieces,
    dual_out,
    dual_in,
    inbound,
    w_sem,
    ag_recv,
    ag_right,
    ag_left,
    rs_recv_r,
    rs_recv_l,
    rs_right,
    rs_left,
    st_send,
    st_recv,
    mk_send,
    mk_recv,
    du_send,
    du_recv,
    ds_send,
    ds_recv,
):
    rows = q_ref.shape[0]
    dk = q_ref.shape[1] // heads
    dv = v_ref.shape[1] // heads
    width = og_ref.shape[1]
    inner = w_ref.shape[0]
    far = levels - near
    spread = n_ctx.bit_length() - 1
    me = lax.axis_index("ctx")
    z = lax.axis_index("head")
    not_first = z > 0
    not_last = z < n_head - 1
    bits = [(me // (1 << s)) % 2 for s in range(spread)]
    partners = [me + (1 - 2 * bits[s]) * (1 << s) for s in range(spread)]

    def remote(src, dst, send, recv, device):
        return pltpu.make_async_remote_copy(
            src_ref=src,
            dst_ref=dst,
            send_sem=send,
            recv_sem=recv,
            device_id=device,
            device_id_type=MESH,
        )

    load = pltpu.make_async_copy(w_hbm, w_ref, w_sem)
    load.start()

    barrier = pltpu.get_barrier_semaphore()
    for s in range(spread):
        pl.semaphore_signal(barrier, inc=1, device_id=(partners[s], z), device_id_type=MESH)

    @pl.when(not_first)
    def _():
        pl.semaphore_signal(barrier, inc=1, device_id=(me, z - 1), device_id_type=MESH)

    @pl.when(not_last)
    def _():
        pl.semaphore_signal(barrier, inc=1, device_id=(me, z + 1), device_id_type=MESH)

    pl.semaphore_wait(
        barrier, spread + not_first.astype(jnp.int32) + not_last.astype(jnp.int32)
    )

    slab = rows // PARTS

    def part_rows(part):
        return pl.ds(part * slab, slab)

    def own_right(part):
        return remote(
            og_ref.at[part_rows(part)],
            gath.at[z, part_rows(part)],
            ag_right.at[z, part],
            ag_recv.at[z, part],
            (me, z + 1),
        )

    def own_left(part):
        return remote(
            og_ref.at[part_rows(part)],
            gath.at[z, part_rows(part)],
            ag_left.at[z, part],
            ag_recv.at[z, part],
            (me, z - 1),
        )

    def pass_right(owner, part):
        block = gath.at[owner, part_rows(part)]
        return remote(
            block, block, ag_right.at[owner, part], ag_recv.at[owner, part], (me, z + 1)
        )

    def pass_left(owner, part):
        block = gath.at[owner, part_rows(part)]
        return remote(block, block, ag_left.at[owner, part], ag_recv.at[owner, part], (me, z - 1))

    for part in range(PARTS):

        @pl.when(not_last)
        def _():
            own_right(part).start()

        @pl.when(not_first)
        def _():
            own_left(part).start()

    def head_k(h):
        return pl.ds(pl.multiple_of(h * dk, dk), dk)

    def head_v(h):
        return pl.ds(pl.multiple_of(h * dv, dv), dv)

    @pl.loop(0, heads)
    def _(h):
        cols = ext_ref[h].T
        cols_ref[h] = cols
        seg = cols[:, levels : levels + 1]
        keep = (seg == seg[rows - 1 : rows, :]).astype(F32)
        masked = (k_ref[:, head_k(h)].astype(F32) * keep).astype(BF16)
        state_out[0, h] = mm(masked, v_ref[:, head_v(h)], 0, 0).astype(BF16)

    seg_row = ext_ref[0, levels : levels + 1, :]
    lane = dv
    first = jnp.broadcast_to(seg_row[:, 0:1], (1, lane))
    last = jnp.broadcast_to(seg_row[:, rows - 1 : rows], (1, lane))
    marks_out[0, 0:8, :] = jnp.broadcast_to(first, (8, lane))
    marks_out[0, 8:16, :] = jnp.broadcast_to(last, (8, lane))

    def hop(s):
        return (
            remote(
                state_out.at[s], state_in.at[s], st_send.at[s], st_recv.at[s], (partners[s], z)
            ),
            remote(
                marks_out.at[s], marks_in.at[s], mk_send.at[s], mk_recv.at[s], (partners[s], z)
            ),
        )

    def hop_start(s):
        for copy in hop(s):
            copy.start()

    def hop_finish(s):
        for copy in hop(s):
            copy.wait_recv()
        up = bits[s].astype(F32)
        own_first, own_last = marks_out[s, 0:1, :], marks_out[s, 8:9, :]
        its_first, its_last = marks_in[s, 0:1, :], marks_in[s, 8:9, :]
        joined = (its_last == own_last).astype(F32)
        linked = (its_last == first).astype(F32) * up
        mine = up + (1 - up) * joined
        theirs = (1 - up) + up * joined
        last_section = s == spread - 1

        @pl.loop(0, heads)
        def _(h):
            partner = state_in[s, h].astype(F32)
            pieces[s, h] = (partner * linked).astype(BF16)
            if not last_section:
                state_out[s + 1, h] = (
                    state_out[s, h].astype(F32) * mine + partner * theirs
                ).astype(BF16)

        if not last_section:
            marks_out[s + 1, 0:8, :] = jnp.broadcast_to(
                up * its_first + (1 - up) * own_first, (8, lane)
            )
            marks_out[s + 1, 8:16, :] = jnp.broadcast_to(
                up * own_last + (1 - up) * its_last, (8, lane)
            )
            hop_start(s + 1)

    if spread:
        hop_start(0)

    table_ref[...] = table(
        cols_ref[0][:, levels : levels + 1], ext_ref[0, levels : levels + 1, :], rows, near
    )
    tile = 256

    def near_forward(low, high):
        @pl.loop(low, high)
        def _(h):
            cols = cols_ref[h]
            level = table_ref[...]
            weight = jnp.zeros((rows, rows), F32)
            for j in range(near):
                weight = jnp.where(level == j, cols[:, j : j + 1], weight)
            weights[h] = weight.astype(BF16)
            p = (weight * mm(q_ref[:, head_k(h)], k_ref[:, head_k(h)], 1, 1)).astype(BF16)
            probs[h] = p
            near_out[:, head_v(h)] = mm(p, v_ref[:, head_v(h)])

    done = 0
    for s in range(spread):
        upto = heads * (s + 1) // spread
        near_forward(done, upto)
        done = upto
        hop_finish(s)
    if done < heads:
        near_forward(done, heads)

    def far_gates(h):
        cols = cols_ref[h]
        seg = cols[:, levels : levels + 1]
        keep = (seg == seg[0:1, :]).astype(F32)
        return [cols[:, near + j : near + j + 1] * keep for j in range(far)]

    @pl.loop(0, heads)
    def _(h):
        gates = far_gates(h)
        q = q_ref[:, head_k(h)]
        out = near_out[:, head_v(h)]
        for j in range(far):
            out = out + gates[j] * mm(q, pieces[j, h])
        mixed_ref[:, head_v(h)] = out.astype(BF16)

    load.wait()

    flip = (z < n_head - z).astype(jnp.int32)

    def project(at):
        dest = flip * (n_head - 1 - at) + (1 - flip) * at

        @pl.loop(0, width // tile)
        def _(c):
            from_col = pl.multiple_of(dest * width + c * tile, tile)
            part = mm(mixed_ref[...], w_ref[:, pl.ds(from_col, tile)])
            pj[dest, :, pl.ds(pl.multiple_of(c * tile, tile), tile)] = part.astype(BF16)

    def product(block, owner, at_rows, fresh):
        @pl.loop(0, inner // tile)
        def _(r):
            at = pl.ds(pl.multiple_of(r * tile, tile), tile)
            term = mm(
                block[at_rows, :],
                w_ref[at, pl.ds(pl.multiple_of(owner * width, width), width)],
                1,
                1,
            )
            acc[at_rows, at] = term if fresh else acc[at_rows, at] + term

    def sum_right(dest, part, src=rsr):
        return remote(
            src.at[dest, part_rows(part)],
            rsr.at[dest, part_rows(part)],
            rs_right.at[dest, part],
            rs_recv_r.at[dest, part],
            (me, z + 1),
        )

    def sum_left(dest, part, src=rsl):
        return remote(
            src.at[dest, part_rows(part)],
            rsl.at[dest, part_rows(part)],
            rs_left.at[dest, part],
            rs_recv_l.at[dest, part],
            (me, z - 1),
        )

    def send_sum(buf, make, has_upstream, dest, part):
        @pl.when(has_upstream)
        def _():
            make(dest, part).wait_recv()

            @pl.loop(0, slab // 64)
            def _(r):
                at = pl.ds(pl.multiple_of(part * slab + r * 64, 64), 64)
                buf[dest, at, :] = (
                    buf[dest, at, :].astype(F32) + pj[dest, at, :].astype(F32)
                ).astype(BF16)

            make(dest, part).start()

        @pl.when(jnp.logical_not(has_upstream))
        def _():
            make(dest, part, pj).start()

    def sums(phase, part):
        reach = n_head - phase

        @pl.when(z + reach < n_head)
        def _():
            send_sum(rsr, sum_right, not_first, z + reach, part)

        @pl.when(z - reach >= 0)
        def _():
            send_sum(rsl, sum_left, not_last, z - reach, part)

    def forwards(phase, part):
        @pl.when(z - phase >= 0)
        def _():
            pass_right(z - phase, part).wait_recv()

            @pl.when(not_last)
            def _():
                pass_right(z - phase, part).start()

        @pl.when(z + phase < n_head)
        def _():
            pass_left(z + phase, part).wait_recv()

            @pl.when(not_first)
            def _():
                pass_left(z + phase, part).start()

    def products(phase, at_rows):
        @pl.when(z - phase >= 0)
        def _():
            product(gath.at[z - phase], z - phase, at_rows, False)

        @pl.when(z + phase < n_head)
        def _():
            product(gath.at[z + phase], z + phase, at_rows, False)

    whole_block = pl.ds(0, rows)
    project(0)
    if n_head > 1:
        for part in range(PARTS):
            sums(1, part)
        project(1)
        for part in range(PARTS):
            forwards(1, part)
    for at in range(2, n_head):
        project(at)
    product(og_ref, z, whole_block, True)
    if n_head > 1:
        products(1, whole_block)
    for phase in range(2, n_head):
        for part in range(PARTS):
            forwards(phase, part)
            sums(phase, part)
            products(phase, part_rows(part))

    @pl.loop(0, heads)
    def _(h):
        g = acc[:, head_v(h)].astype(BF16)
        cot[:, head_v(h)] = g
        g = g.astype(F32)
        q = q_ref[:, head_k(h)]
        gates = far_gates(h)
        for j in range(far):
            dual_out[j, h] = mm(q, (g * gates[j]).astype(BF16), 0, 0).astype(BF16)

    starts = [sum(spread - i for i in range(s)) for s in range(spread + 1)]

    split = heads // 2 if heads % 2 == 0 else 0

    def dual_hop(s):
        block = pl.ds(starts[s], spread - s)
        if s and split:
            block = (block, pl.ds(bits[0] * split, split))
        return remote(
            dual_out.at[block], dual_in.at[block], du_send.at[s], du_recv.at[s], (partners[s], z)
        )

    def dual_share(s):
        block = (pl.ds(starts[s], spread - s), pl.ds(bits[0] * split, split))
        return remote(
            dual_in.at[block], dual_in.at[block], ds_send.at[s], ds_recv.at[s], (partners[0], z)
        )

    def dual_finish(s):
        dual_hop(s).wait_recv()
        if s and split:
            dual_share(s).start()
            dual_share(s).wait_recv()
        up = bits[s].astype(F32)
        own_first, its_first = marks_out[s, 0:1, :], marks_in[s, 0:1, :]
        joined = (its_first == own_first).astype(F32)
        linked = (its_first == last).astype(F32) * (1 - up)
        mine = (1 - up) + up * joined
        theirs = up + (1 - up) * joined

        @pl.loop(0, heads)
        def _(h):
            gain = dual_in[starts[s], h].astype(F32) * linked
            inbound[h] = gain if s == 0 else inbound[h] + gain
            for j in range(1, spread - s):
                dual_out[starts[s + 1] + j - 1, h] = (
                    dual_out[starts[s] + j, h].astype(F32) * mine
                    + dual_in[starts[s] + j, h].astype(F32) * theirs
                ).astype(BF16)

        if s < spread - 1:
            dual_hop(s + 1).start()

    if spread:
        dual_hop(0).start()

    def near_backward(low, high):
        @pl.loop(low, high)
        def _(h):
            q, k = q_ref[:, head_k(h)], k_ref[:, head_k(h)]
            v, g = v_ref[:, head_v(h)], cot[:, head_v(h)]
            near_out[:, head_v(h)] = mm(probs[h], g, 0, 0)
            grads = (weights[h].astype(F32) * mm(g, v, 1, 1)).astype(BF16)
            acc[:, head_k(h)] = mm(grads, q, 0, 0)
            dq = mm(grads, k)
            gates = far_gates(h)
            for j in range(far):
                dq = dq + gates[j] * mm(g, pieces[j, h], 1, 1)
            dq_ref[:, head_k(h)] = dq.astype(BF16)

    done = 0
    for s in range(spread):
        upto = heads * (s + 1) // spread
        near_backward(done, upto)
        done = upto
        dual_finish(s)
    if done < heads:
        near_backward(done, heads)

    @pl.loop(0, heads)
    def _(h):
        seg = cols_ref[h][:, levels : levels + 1]
        keep = (seg == seg[rows - 1 : rows, :]).astype(F32)
        near_dk, near_dv = acc[:, head_k(h)], near_out[:, head_v(h)]
        if spread:
            state = inbound[h].astype(BF16)
            near_dk = near_dk + keep * mm(v_ref[:, head_v(h)], state, 1, 1)
            near_dv = near_dv + keep * mm(k_ref[:, head_k(h)], state)
        dk_ref[:, head_k(h)] = near_dk.astype(BF16)
        dv_ref[:, head_v(h)] = near_dv.astype(BF16)

    acc[...] = pj[z].astype(F32)

    @pl.when(not_first)
    def _():
        for part in range(PARTS):
            sum_right(z, part).wait_recv()
        acc[...] = acc[...] + rsr[z].astype(F32)

    @pl.when(not_last)
    def _():
        for part in range(PARTS):
            sum_left(z, part).wait_recv()
        acc[...] = acc[...] + rsl[z].astype(F32)

    mixed_ref[...] = acc[...].astype(BF16)

    for part in range(PARTS):

        @pl.when(not_last)
        def _():
            own_right(part).wait_send()

        @pl.when(not_first)
        def _():
            own_left(part).wait_send()

        for phase in range(1, n_head):
            reach = n_head - phase

            @pl.when((z - phase >= 0) & not_last)
            def _():
                pass_right(z - phase, part).wait_send()

            @pl.when((z + phase < n_head) & not_first)
            def _():
                pass_left(z + phase, part).wait_send()

            @pl.when(z + reach < n_head)
            def _():
                sum_right(z + reach, part).wait_send()

            @pl.when(z - reach >= 0)
            def _():
                sum_left(z - reach, part).wait_send()

    for s in range(spread):
        for copy in hop(s):
            copy.wait_send()
        dual_hop(s).wait_send()
        if s and split:
            dual_share(s).wait_send()


def shards(queries, keys, values, gates, segment_ids, out_weight, out_grad):
    rows = queries.shape[0]
    heads, levels = gates.shape[0], gates.shape[1]
    dk = queries.shape[1] // heads
    dv = values.shape[1] // heads
    near = (rows // SPAN).bit_length()
    n_ctx = lax.axis_size("ctx")
    n_head = lax.axis_size("head")
    spread = n_ctx.bit_length() - 1
    width = out_grad.shape[1]
    inner = out_weight.shape[0]
    size = -(-(levels + 1) // 8) * 8
    ext = jnp.concatenate(
        [
            gates,
            jnp.broadcast_to(segment_ids.astype(F32), (heads, 1, rows)),
            jnp.zeros((heads, size - levels - 1, rows), F32),
        ],
        axis=1,
    )
    duals = max(spread * (spread + 1) // 2, 1)
    hops = max(spread, 1)
    dma = pltpu.SemaphoreType.DMA
    vmem = pl.BlockSpec(memory_space=pltpu.VMEM)
    return pl.pallas_call(
        functools.partial(kernel, n_ctx, n_head, heads, levels, near),
        in_specs=[vmem] * 5 + [pl.BlockSpec(memory_space=pl.ANY)],
        out_specs=[vmem] * 4,
        out_shape=[
            jax.ShapeDtypeStruct((rows, width), BF16),
            jax.ShapeDtypeStruct(queries.shape, BF16),
            jax.ShapeDtypeStruct(keys.shape, BF16),
            jax.ShapeDtypeStruct(values.shape, BF16),
        ],
        scratch_shapes=[
            pltpu.VMEM(out_weight.shape, BF16),
            pltpu.VMEM((n_head, rows, width), BF16),
            pltpu.VMEM((rows, inner), F32),
            pltpu.VMEM((rows, inner), F32),
            pltpu.VMEM((n_head, rows, width), BF16),
            pltpu.VMEM((n_head, rows, width), BF16),
            pltpu.VMEM((n_head, rows, width), BF16),
            pltpu.VMEM((heads, rows, rows), BF16),
            pltpu.VMEM((heads, rows, rows), BF16),
            pltpu.VMEM((rows, rows), jnp.int32),
            pltpu.VMEM((heads, rows, size), F32),
            pltpu.VMEM((rows, inner), BF16),
            pltpu.VMEM((hops, heads, dk, dv), BF16),
            pltpu.VMEM((hops, heads, dk, dv), BF16),
            pltpu.VMEM((hops, 16, dv), F32),
            pltpu.VMEM((hops, 16, dv), F32),
            pltpu.VMEM((hops, heads, dk, dv), BF16),
            pltpu.VMEM((duals, heads, dk, dv), BF16),
            pltpu.VMEM((duals, heads, dk, dv), BF16),
            pltpu.VMEM((heads, dk, dv), F32),
            dma,
            dma((n_head, PARTS)),
            dma((n_head, PARTS)),
            dma((n_head, PARTS)),
            dma((n_head, PARTS)),
            dma((n_head, PARTS)),
            dma((n_head, PARTS)),
            dma((n_head, PARTS)),
            dma((hops,)),
            dma((hops,)),
            dma((hops,)),
            dma((hops,)),
            dma((hops,)),
            dma((hops,)),
            dma((hops,)),
            dma((hops,)),
        ],
        compiler_params=pltpu.CompilerParams(
            collective_id=0, has_side_effects=True, vmem_limit_bytes=60 << 20
        ),
        cost_estimate=pl.CostEstimate(
            flops=4 * rows * n_head * width * inner + 14 * rows * rows * dk * heads,
            bytes_accessed=40 << 20,
            transcendentals=0,
        ),
    )(queries, keys, values, out_grad, ext, out_weight)


def copy_kernel(*refs):
    half = len(refs) // 2
    for source, target in zip(refs[:half], refs[half:]):
        target[...] = source[...]


def results(arrays):
    spec = [pl.BlockSpec((a.shape[0] // 4, a.shape[1]), lambda i: (i, 0)) for a in arrays]
    return tuple(
        pl.pallas_call(
            copy_kernel,
            grid=(4,),
            in_specs=spec,
            out_specs=spec,
            out_shape=[jax.ShapeDtypeStruct(a.shape, a.dtype) for a in arrays],
            compiler_params=pltpu.CompilerParams(vmem_limit_bytes=60 << 20),
        )(*arrays)
    )


def solution(mesh):
    placed = (
        P("ctx", "head"),
        P("ctx", "head"),
        P("ctx", "head"),
        P("head", None, "ctx"),
        P("ctx"),
        P("head", None),
        P("ctx", "head"),
    )

    def body(*args):
        return results(shards(*args))

    return jax.shard_map(
        body,
        mesh=mesh,
        in_specs=placed,
        out_specs=(P("ctx", "head"), P("ctx", "head"), P("ctx", "head"), P("ctx", "head")),
        check_vma=False,
    )
```

```python
import functools

import jax
import jax.numpy as jnp
from jax import lax
from jax.experimental import pallas as pl
from jax.experimental.pallas import tpu as pltpu
from jax.sharding import PartitionSpec as P

SPAN = 64
PARTS = 2
F32 = jnp.float32
BF16 = jnp.bfloat16
MESH = pl.DeviceIdType.MESH


def mm(a, b, ca=1, cb=0):
    return lax.dot_general(a, b, (((ca,), (cb,)), ((), ())), preferred_element_type=F32)


def table(seg_col, seg_row, rows, near):
    t = lax.broadcasted_iota(jnp.int32, (rows, rows), 0)
    s = lax.broadcasted_iota(jnp.int32, (rows, rows), 1)
    differ = jnp.bitwise_xor(t // SPAN, s // SPAN)
    level = jnp.zeros((rows, rows), jnp.int32)
    for section in range(near - 1):
        level = level + (differ >= 1 << section).astype(jnp.int32)
    return jnp.where((t >= s) & (seg_col == seg_row), level, near)


def kernel(
    n_ctx,
    n_head,
    heads,
    levels,
    near,
    q_hbm,
    k_hbm,
    v_hbm,
    og_hbm,
    w_hbm,
    gates_ref,
    seg_ref,
    mixed_hbm,
    dq_hbm,
    dk_hbm,
    dv_hbm,
    q_ref,
    k_ref,
    v_ref,
    og_ref,
    mixed_ref,
    dq_ref,
    dk_ref,
    dv_ref,
    ext_ref,
    leaf_acc,
    w_ref,
    gath,
    acc,
    near_out,
    pj,
    rsr,
    rsl,
    weights,
    probs,
    table_ref,
    cols_ref,
    cot,
    state_out,
    state_in,
    marks_out,
    marks_in,
    pieces,
    dual_out,
    dual_in,
    inbound,
    in_sem,
    out_sem,
    ag_recv,
    ag_right,
    ag_left,
    rs_recv_r,
    rs_recv_l,
    rs_right,
    rs_left,
    st_send,
    st_recv,
    mk_send,
    mk_recv,
    du_send,
    du_recv,
    ds_send,
    ds_recv,
):
    rows = q_ref.shape[0]
    dk = q_ref.shape[1] // heads
    dv = v_ref.shape[1] // heads
    width = og_ref.shape[1]
    inner = w_ref.shape[0]
    far = levels - near
    spread = n_ctx.bit_length() - 1
    me = lax.axis_index("ctx")
    z = lax.axis_index("head")
    not_first = z > 0
    not_last = z < n_head - 1
    bits = [(me // (1 << s)) % 2 for s in range(spread)]
    partners = [me + (1 - 2 * bits[s]) * (1 << s) for s in range(spread)]

    def remote(src, dst, send, recv, device):
        return pltpu.make_async_remote_copy(
            src_ref=src,
            dst_ref=dst,
            send_sem=send,
            recv_sem=recv,
            device_id=device,
            device_id_type=MESH,
        )

    loads = [
        pltpu.make_async_copy(source, target, in_sem.at[i])
        for i, (source, target) in enumerate(
            ((k_hbm, k_ref), (v_hbm, v_ref), (q_hbm, q_ref), (og_hbm, og_ref), (w_hbm, w_ref))
        )
    ]
    barrier = pltpu.get_barrier_semaphore()
    for s in range(spread):
        pl.semaphore_signal(barrier, inc=1, device_id=(partners[s], z), device_id_type=MESH)

    @pl.when(not_first)
    def _():
        pl.semaphore_signal(barrier, inc=1, device_id=(me, z - 1), device_id_type=MESH)

    @pl.when(not_last)
    def _():
        pl.semaphore_signal(barrier, inc=1, device_id=(me, z + 1), device_id_type=MESH)

    for load in loads:
        load.start()

    for j in range(levels):
        ext_ref[:, j, :] = gates_ref[j]
    for j in range(levels, ext_ref.shape[1]):
        ext_ref[:, j, :] = jnp.broadcast_to(seg_ref[...].astype(F32), (heads, rows))

    pl.semaphore_wait(
        barrier, spread + not_first.astype(jnp.int32) + not_last.astype(jnp.int32)
    )

    slab = rows // PARTS

    def part_rows(part):
        return pl.ds(part * slab, slab)

    def own_right(part):
        return remote(
            og_hbm.at[part_rows(part)],
            gath.at[z, part_rows(part)],
            ag_right.at[z, part],
            ag_recv.at[z, part],
            (me, z + 1),
        )

    def own_left(part):
        return remote(
            og_hbm.at[part_rows(part)],
            gath.at[z, part_rows(part)],
            ag_left.at[z, part],
            ag_recv.at[z, part],
            (me, z - 1),
        )

    def pass_right(owner, part):
        block = gath.at[owner, part_rows(part)]
        return remote(
            block, block, ag_right.at[owner, part], ag_recv.at[owner, part], (me, z + 1)
        )

    def pass_left(owner, part):
        block = gath.at[owner, part_rows(part)]
        return remote(block, block, ag_left.at[owner, part], ag_recv.at[owner, part], (me, z - 1))

    for part in range(PARTS):

        @pl.when(not_last)
        def _():
            own_right(part).start()

        @pl.when(not_first)
        def _():
            own_left(part).start()

    def head_k(h):
        return pl.ds(pl.multiple_of(h * dk, dk), dk)

    def head_v(h):
        return pl.ds(pl.multiple_of(h * dv, dv), dv)

    loads[0].wait()
    loads[1].wait()

    @pl.loop(0, heads)
    def _(h):
        cols = ext_ref[h].T
        cols_ref[h] = cols
        seg = cols[:, levels : levels + 1]
        keep = (seg == seg[rows - 1 : rows, :]).astype(F32)
        masked = (k_ref[:, head_k(h)].astype(F32) * keep).astype(BF16)
        state_out[0, h] = mm(masked, v_ref[:, head_v(h)], 0, 0).astype(BF16)

    seg_row = ext_ref[0, levels : levels + 1, :]
    lane = dv
    first = jnp.broadcast_to(seg_row[:, 0:1], (1, lane))
    last = jnp.broadcast_to(seg_row[:, rows - 1 : rows], (1, lane))
    marks_out[0, 0:8, :] = jnp.broadcast_to(first, (8, lane))
    marks_out[0, 8:16, :] = jnp.broadcast_to(last, (8, lane))

    def hop(s):
        return (
            remote(
                state_out.at[s], state_in.at[s], st_send.at[s], st_recv.at[s], (partners[s], z)
            ),
            remote(
                marks_out.at[s], marks_in.at[s], mk_send.at[s], mk_recv.at[s], (partners[s], z)
            ),
        )

    def hop_start(s):
        for copy in hop(s):
            copy.start()

    def hop_finish(s):
        for copy in hop(s):
            copy.wait_recv()
        up = bits[s].astype(F32)
        own_first, own_last = marks_out[s, 0:1, :], marks_out[s, 8:9, :]
        its_first, its_last = marks_in[s, 0:1, :], marks_in[s, 8:9, :]
        joined = (its_last == own_last).astype(F32)
        linked = (its_last == first).astype(F32) * up
        mine = up + (1 - up) * joined
        theirs = (1 - up) + up * joined
        last_section = s == spread - 1

        @pl.loop(0, heads)
        def _(h):
            partner = state_in[s, h].astype(F32)
            pieces[s, h] = (partner * linked).astype(BF16)
            if not last_section:
                state_out[s + 1, h] = (
                    state_out[s, h].astype(F32) * mine + partner * theirs
                ).astype(BF16)

        if not last_section:
            marks_out[s + 1, 0:8, :] = jnp.broadcast_to(
                up * its_first + (1 - up) * own_first, (8, lane)
            )
            marks_out[s + 1, 8:16, :] = jnp.broadcast_to(
                up * own_last + (1 - up) * its_last, (8, lane)
            )
            hop_start(s + 1)

    if spread:
        hop_start(0)

    table_ref[...] = table(
        cols_ref[0][:, levels : levels + 1], ext_ref[0, levels : levels + 1, :], rows, near
    )
    tile = 256
    loads[2].wait()

    def near_forward(low, high):
        @pl.loop(low, high)
        def _(h):
            cols = cols_ref[h]
            level = table_ref[...]
            weight = jnp.zeros((rows, rows), F32)
            for j in range(near):
                weight = jnp.where(level == j, cols[:, j : j + 1], weight)
            weights[h] = weight.astype(BF16)
            p = (weight * mm(q_ref[:, head_k(h)], k_ref[:, head_k(h)], 1, 1)).astype(BF16)
            probs[h] = p
            near_out[:, head_v(h)] = mm(p, v_ref[:, head_v(h)])

    done = 0
    for s in range(spread):
        upto = heads * (s + 1) // spread
        near_forward(done, upto)
        done = upto
        hop_finish(s)
    if done < heads:
        near_forward(done, heads)

    def far_gates(h):
        cols = cols_ref[h]
        seg = cols[:, levels : levels + 1]
        keep = (seg == seg[0:1, :]).astype(F32)
        return [cols[:, near + j : near + j + 1] * keep for j in range(far)]

    @pl.loop(0, heads)
    def _(h):
        gates = far_gates(h)
        q = q_ref[:, head_k(h)]
        out = near_out[:, head_v(h)]
        for j in range(far):
            out = out + gates[j] * mm(q, pieces[j, h])
        mixed_ref[:, head_v(h)] = out.astype(BF16)

    loads[3].wait()
    loads[4].wait()

    flip = (z < n_head - z).astype(jnp.int32)

    def project(at):
        dest = flip * (n_head - 1 - at) + (1 - flip) * at

        @pl.loop(0, width // tile)
        def _(c):
            from_col = pl.multiple_of(dest * width + c * tile, tile)
            part = mm(mixed_ref[...], w_ref[:, pl.ds(from_col, tile)])
            pj[dest, :, pl.ds(pl.multiple_of(c * tile, tile), tile)] = part.astype(BF16)

    def product(block, owner, at_rows, fresh):
        @pl.loop(0, inner // tile)
        def _(r):
            at = pl.ds(pl.multiple_of(r * tile, tile), tile)
            term = mm(
                block[at_rows, :],
                w_ref[at, pl.ds(pl.multiple_of(owner * width, width), width)],
                1,
                1,
            )
            acc[at_rows, at] = term if fresh else acc[at_rows, at] + term

    def sum_right(dest, part, src=rsr):
        return remote(
            src.at[dest, part_rows(part)],
            rsr.at[dest, part_rows(part)],
            rs_right.at[dest, part],
            rs_recv_r.at[dest, part],
            (me, z + 1),
        )

    def sum_left(dest, part, src=rsl):
        return remote(
            src.at[dest, part_rows(part)],
            rsl.at[dest, part_rows(part)],
            rs_left.at[dest, part],
            rs_recv_l.at[dest, part],
            (me, z - 1),
        )

    def send_sum(buf, make, has_upstream, dest, part):
        @pl.when(has_upstream)
        def _():
            make(dest, part).wait_recv()

            @pl.loop(0, slab // 64)
            def _(r):
                at = pl.ds(pl.multiple_of(part * slab + r * 64, 64), 64)
                buf[dest, at, :] = (
                    buf[dest, at, :].astype(F32) + pj[dest, at, :].astype(F32)
                ).astype(BF16)

            make(dest, part).start()

        @pl.when(jnp.logical_not(has_upstream))
        def _():
            make(dest, part, pj).start()

    def sums(phase, part):
        reach = n_head - phase

        @pl.when(z + reach < n_head)
        def _():
            send_sum(rsr, sum_right, not_first, z + reach, part)

        @pl.when(z - reach >= 0)
        def _():
            send_sum(rsl, sum_left, not_last, z - reach, part)

    def forwards(phase, part):
        @pl.when(z - phase >= 0)
        def _():
            pass_right(z - phase, part).wait_recv()

            @pl.when(not_last)
            def _():
                pass_right(z - phase, part).start()

        @pl.when(z + phase < n_head)
        def _():
            pass_left(z + phase, part).wait_recv()

            @pl.when(not_first)
            def _():
                pass_left(z + phase, part).start()

    def products(phase, at_rows):
        @pl.when(z - phase >= 0)
        def _():
            product(gath.at[z - phase], z - phase, at_rows, False)

        @pl.when(z + phase < n_head)
        def _():
            product(gath.at[z + phase], z + phase, at_rows, False)

    def leaves(part):
        at = part_rows(part)

        @pl.loop(0, heads)
        def _(h):
            g = acc[at, head_v(h)].astype(BF16)
            cot[at, head_v(h)] = g
            g = g.astype(F32)
            q = q_ref[at, head_k(h)]
            gates = far_gates(h)
            for j in range(far):
                term = mm(q, (g * gates[j][part * slab : (part + 1) * slab]).astype(BF16), 0, 0)
                if part:
                    term = leaf_acc[j, h] + term
                if part < PARTS - 1:
                    leaf_acc[j, h] = term
                else:
                    dual_out[j, h] = term.astype(BF16)

    whole_block = pl.ds(0, rows)
    project(0)
    if n_head > 1:
        for part in range(PARTS):
            sums(1, part)
        project(1)
        for part in range(PARTS):
            forwards(1, part)
    for at in range(2, n_head):
        project(at)
    product(og_ref, z, whole_block, True)
    if n_head > 1:
        products(1, whole_block)
    for phase in range(2, n_head):
        for part in range(PARTS):
            forwards(phase, part)
            sums(phase, part)
            products(phase, part_rows(part))
            if phase == n_head - 1:
                leaves(part)
    if n_head < 3:
        for part in range(PARTS):
            leaves(part)

    starts = [sum(spread - i for i in range(s)) for s in range(spread + 1)]

    split = heads // 2 if heads % 2 == 0 else 0

    def dual_hop(s):
        block = pl.ds(starts[s], spread - s)
        if s and split:
            block = (block, pl.ds(bits[0] * split, split))
        return remote(
            dual_out.at[block], dual_in.at[block], du_send.at[s], du_recv.at[s], (partners[s], z)
        )

    def dual_share(s):
        block = (pl.ds(starts[s], spread - s), pl.ds(bits[0] * split, split))
        return remote(
            dual_in.at[block], dual_in.at[block], ds_send.at[s], ds_recv.at[s], (partners[0], z)
        )

    def dual_finish(s):
        dual_hop(s).wait_recv()
        if s and split:
            dual_share(s).start()
            dual_share(s).wait_recv()
        up = bits[s].astype(F32)
        own_first, its_first = marks_out[s, 0:1, :], marks_in[s, 0:1, :]
        joined = (its_first == own_first).astype(F32)
        linked = (its_first == last).astype(F32) * (1 - up)
        mine = (1 - up) + up * joined
        theirs = up + (1 - up) * joined

        @pl.loop(0, heads)
        def _(h):
            gain = dual_in[starts[s], h].astype(F32) * linked
            inbound[h] = gain if s == 0 else inbound[h] + gain
            for j in range(1, spread - s):
                dual_out[starts[s + 1] + j - 1, h] = (
                    dual_out[starts[s] + j, h].astype(F32) * mine
                    + dual_in[starts[s] + j, h].astype(F32) * theirs
                ).astype(BF16)

        if s < spread - 1:
            dual_hop(s + 1).start()

    if spread:
        dual_hop(0).start()

    stores = [
        pltpu.make_async_copy(source, target, out_sem.at[i])
        for i, (source, target) in enumerate(((dq_ref, dq_hbm), (dk_ref, dk_hbm), (dv_ref, dv_hbm)))
    ]

    def near_backward(low, high):
        @pl.loop(low, high)
        def _(h):
            q, k = q_ref[:, head_k(h)], k_ref[:, head_k(h)]
            v, g = v_ref[:, head_v(h)], cot[:, head_v(h)]
            near_out[:, head_v(h)] = mm(probs[h], g, 0, 0)
            grads = (weights[h].astype(F32) * mm(g, v, 1, 1)).astype(BF16)
            acc[:, head_k(h)] = mm(grads, q, 0, 0)
            dq = mm(grads, k)
            gates = far_gates(h)
            for j in range(far):
                dq = dq + gates[j] * mm(g, pieces[j, h], 1, 1)
            dq_ref[:, head_k(h)] = dq.astype(BF16)

    done = 0
    for s in range(spread):
        upto = heads * (s + 1) // spread
        near_backward(done, upto)
        done = upto
        dual_finish(s)
    if done < heads:
        near_backward(done, heads)
    stores[0].start()

    @pl.loop(0, heads)
    def _(h):
        seg = cols_ref[h][:, levels : levels + 1]
        keep = (seg == seg[rows - 1 : rows, :]).astype(F32)
        near_dk, near_dv = acc[:, head_k(h)], near_out[:, head_v(h)]
        if spread:
            state = inbound[h].astype(BF16)
            near_dk = near_dk + keep * mm(v_ref[:, head_v(h)], state, 1, 1)
            near_dv = near_dv + keep * mm(k_ref[:, head_k(h)], state)
        dk_ref[:, head_k(h)] = near_dk.astype(BF16)
        dv_ref[:, head_v(h)] = near_dv.astype(BF16)

    stores[1].start()
    stores[2].start()

    def last_sum(part, upstream):
        @pl.loop(0, slab // 64)
        def _(r):
            at = pl.ds(pl.multiple_of(part * slab + r * 64, 64), 64)
            total = pj[z, at, :].astype(F32)
            for buf in upstream:
                total = total + buf[z, at, :].astype(F32)
            mixed_ref[at, :] = total.astype(BF16)

    def mixed_store(part):
        return pltpu.make_async_copy(
            mixed_ref.at[part_rows(part)], mixed_hbm.at[part_rows(part)], out_sem.at[3 + part]
        )

    for part in range(PARTS):

        @pl.when(not_first)
        def _():
            sum_right(z, part).wait_recv()

        @pl.when(not_last)
        def _():
            sum_left(z, part).wait_recv()

        @pl.when(not_first & not_last)
        def _():
            last_sum(part, (rsr, rsl))

        @pl.when(not_first & jnp.logical_not(not_last))
        def _():
            last_sum(part, (rsr,))

        @pl.when(not_last & jnp.logical_not(not_first))
        def _():
            last_sum(part, (rsl,))

        if n_head == 1:
            last_sum(part, ())
        mixed_store(part).start()

    for part in range(PARTS):

        @pl.when(not_last)
        def _():
            own_right(part).wait_send()

        @pl.when(not_first)
        def _():
            own_left(part).wait_send()

        for phase in range(1, n_head):
            reach = n_head - phase

            @pl.when((z - phase >= 0) & not_last)
            def _():
                pass_right(z - phase, part).wait_send()

            @pl.when((z + phase < n_head) & not_first)
            def _():
                pass_left(z + phase, part).wait_send()

            @pl.when(z + reach < n_head)
            def _():
                sum_right(z + reach, part).wait_send()

            @pl.when(z - reach >= 0)
            def _():
                sum_left(z - reach, part).wait_send()

    for s in range(spread):
        for copy in hop(s):
            copy.wait_send()
        dual_hop(s).wait_send()
        if s and split:
            dual_share(s).wait_send()
    for store in stores:
        store.wait()
    for part in range(PARTS):
        mixed_store(part).wait()


def shards(queries, keys, values, gates, segment_ids, out_weight, out_grad):
    rows = queries.shape[0]
    heads, levels = gates.shape[0], gates.shape[1]
    dk = queries.shape[1] // heads
    dv = values.shape[1] // heads
    near = (rows // SPAN).bit_length()
    n_ctx = lax.axis_size("ctx")
    n_head = lax.axis_size("head")
    spread = n_ctx.bit_length() - 1
    width = out_grad.shape[1]
    inner = out_weight.shape[0]
    size = -(-(levels + 1) // 8) * 8
    duals = max(spread * (spread + 1) // 2, 1)
    hops = max(spread, 1)
    dma = pltpu.SemaphoreType.DMA
    vmem = pl.BlockSpec(memory_space=pltpu.VMEM)
    hbm = pl.BlockSpec(memory_space=pl.ANY)
    return pl.pallas_call(
        functools.partial(kernel, n_ctx, n_head, heads, levels, near),
        in_specs=[hbm] * 5 + [vmem] * 2,
        out_specs=[hbm] * 4,
        out_shape=[
            jax.ShapeDtypeStruct((rows, width), BF16),
            jax.ShapeDtypeStruct(queries.shape, BF16),
            jax.ShapeDtypeStruct(keys.shape, BF16),
            jax.ShapeDtypeStruct(values.shape, BF16),
        ],
        scratch_shapes=[
            pltpu.VMEM(queries.shape, BF16),
            pltpu.VMEM(keys.shape, BF16),
            pltpu.VMEM(values.shape, BF16),
            pltpu.VMEM(out_grad.shape, BF16),
            pltpu.VMEM((rows, max(width, inner)), BF16),
            pltpu.VMEM(queries.shape, BF16),
            pltpu.VMEM(keys.shape, BF16),
            pltpu.VMEM(values.shape, BF16),
            pltpu.VMEM((heads, size, rows), F32),
            pltpu.VMEM((levels - near, heads, dk, dv), F32),
            pltpu.VMEM(out_weight.shape, BF16),
            pltpu.VMEM((n_head, rows, width), BF16),
            pltpu.VMEM((rows, inner), F32),
            pltpu.VMEM((rows, inner), F32),
            pltpu.VMEM((n_head, rows, width), BF16),
            pltpu.VMEM((n_head, rows, width), BF16),
            pltpu.VMEM((n_head, rows, width), BF16),
            pltpu.VMEM((heads, rows, rows), BF16),
            pltpu.VMEM((heads, rows, rows), BF16),
            pltpu.VMEM((rows, rows), jnp.int32),
            pltpu.VMEM((heads, rows, size), F32),
            pltpu.VMEM((rows, inner), BF16),
            pltpu.VMEM((hops, heads, dk, dv), BF16),
            pltpu.VMEM((hops, heads, dk, dv), BF16),
            pltpu.VMEM((hops, 16, dv), F32),
            pltpu.VMEM((hops, 16, dv), F32),
            pltpu.VMEM((hops, heads, dk, dv), BF16),
            pltpu.VMEM((duals, heads, dk, dv), BF16),
            pltpu.VMEM((duals, heads, dk, dv), BF16),
            pltpu.VMEM((heads, dk, dv), F32),
            dma((5,)),
            dma((3 + PARTS,)),
            dma((n_head, PARTS)),
            dma((n_head, PARTS)),
            dma((n_head, PARTS)),
            dma((n_head, PARTS)),
            dma((n_head, PARTS)),
            dma((n_head, PARTS)),
            dma((n_head, PARTS)),
            dma((hops,)),
            dma((hops,)),
            dma((hops,)),
            dma((hops,)),
            dma((hops,)),
            dma((hops,)),
            dma((hops,)),
            dma((hops,)),
        ],
        compiler_params=pltpu.CompilerParams(
            collective_id=0, has_side_effects=True, vmem_limit_bytes=60 << 20
        ),
        cost_estimate=pl.CostEstimate(
            flops=4 * rows * n_head * width * inner + 14 * rows * rows * dk * heads,
            bytes_accessed=40 << 20,
            transcendentals=0,
        ),
    )(
        queries,
        keys,
        values,
        out_grad,
        out_weight,
        gates.transpose(1, 0, 2),
        segment_ids.reshape(1, rows),
    )


def copy_kernel(*refs):
    sems, refs = refs[-1], refs[:-1]
    half = len(refs) // 2
    copies = []
    for i in range(half):
        slab = refs[i].shape[0] // 4
        for j in range(4):
            at = pl.ds(j * slab, slab)
            copies.append(
                pltpu.make_async_copy(refs[i].at[at], refs[half + i].at[at], sems.at[4 * i + j])
            )
    for copy in copies:
        copy.start()
    for copy in copies:
        copy.wait()


def results(arrays):
    spec = [pl.BlockSpec(memory_space=pl.ANY)] * len(arrays)
    return tuple(
        pl.pallas_call(
            copy_kernel,
            in_specs=spec,
            out_specs=spec,
            out_shape=[jax.ShapeDtypeStruct(a.shape, a.dtype) for a in arrays],
            scratch_shapes=[pltpu.SemaphoreType.DMA((4 * len(arrays),))],
            compiler_params=pltpu.CompilerParams(vmem_limit_bytes=60 << 20),
        )(*arrays)
    )


def solution(mesh):
    placed = (
        P("ctx", "head"),
        P("ctx", "head"),
        P("ctx", "head"),
        P("head", None, "ctx"),
        P("ctx"),
        P("head", None),
        P("ctx", "head"),
    )

    def body(*args):
        return results(shards(*args))

    return jax.shard_map(
        body,
        mesh=mesh,
        in_specs=placed,
        out_specs=(P("ctx", "head"), P("ctx", "head"), P("ctx", "head"), P("ctx", "head")),
        check_vma=False,
    )
```

```python
import functools

import jax
import jax.numpy as jnp
from jax import lax
from jax.experimental import pallas as pl
from jax.experimental.pallas import tpu as pltpu
from jax.sharding import PartitionSpec as P

SPAN = 64
PARTS = 2
F32 = jnp.float32
BF16 = jnp.bfloat16
MESH = pl.DeviceIdType.MESH


def mm(a, b, ca=1, cb=0):
    return lax.dot_general(a, b, (((ca,), (cb,)), ((), ())), preferred_element_type=F32)


def table(seg_col, seg_row, rows, near):
    t = lax.broadcasted_iota(jnp.int32, (rows, rows), 0)
    s = lax.broadcasted_iota(jnp.int32, (rows, rows), 1)
    differ = jnp.bitwise_xor(t // SPAN, s // SPAN)
    level = jnp.zeros((rows, rows), jnp.int32)
    for section in range(near - 1):
        level = level + (differ >= 1 << section).astype(jnp.int32)
    return jnp.where((t >= s) & (seg_col == seg_row), level, near)


def kernel(
    n_ctx,
    n_head,
    heads,
    levels,
    near,
    q_hbm,
    k_hbm,
    v_hbm,
    og_hbm,
    w_hbm,
    gates_ref,
    seg_ref,
    mixed_hbm,
    dq_hbm,
    dk_hbm,
    dv_hbm,
    q_ref,
    k_ref,
    v_ref,
    og_ref,
    mixed_ref,
    dq_ref,
    dk_ref,
    dv_ref,
    ext_ref,
    leaf_acc,
    w_ref,
    gath,
    acc,
    near_out,
    pj,
    rsr,
    rsl,
    weights,
    probs,
    table_ref,
    cols_ref,
    cot,
    state_out,
    state_in,
    marks_out,
    marks_in,
    pieces,
    dual_out,
    dual_in,
    inbound,
    in_sem,
    out_sem,
    ag_recv,
    ag_right,
    ag_left,
    rs_recv_r,
    rs_recv_l,
    rs_right,
    rs_left,
    st_send,
    st_recv,
    mk_send,
    mk_recv,
    du_send,
    du_recv,
    ds_send,
    ds_recv,
    fs_send,
    fs_recv,
):
    rows = q_ref.shape[0]
    dk = q_ref.shape[1] // heads
    dv = v_ref.shape[1] // heads
    width = og_ref.shape[1]
    inner = w_ref.shape[0]
    far = levels - near
    spread = n_ctx.bit_length() - 1
    me = lax.axis_index("ctx")
    z = lax.axis_index("head")
    not_first = z > 0
    not_last = z < n_head - 1
    bits = [(me // (1 << s)) % 2 for s in range(spread)]
    partners = [me + (1 - 2 * bits[s]) * (1 << s) for s in range(spread)]

    def remote(src, dst, send, recv, device):
        return pltpu.make_async_remote_copy(
            src_ref=src,
            dst_ref=dst,
            send_sem=send,
            recv_sem=recv,
            device_id=device,
            device_id_type=MESH,
        )

    loads = [
        pltpu.make_async_copy(source, target, in_sem.at[i])
        for i, (source, target) in enumerate(
            ((k_hbm, k_ref), (v_hbm, v_ref), (q_hbm, q_ref), (og_hbm, og_ref), (w_hbm, w_ref))
        )
    ]
    barrier = pltpu.get_barrier_semaphore()
    for s in range(spread):
        pl.semaphore_signal(barrier, inc=1, device_id=(partners[s], z), device_id_type=MESH)

    @pl.when(not_first)
    def _():
        pl.semaphore_signal(barrier, inc=1, device_id=(me, z - 1), device_id_type=MESH)

    @pl.when(not_last)
    def _():
        pl.semaphore_signal(barrier, inc=1, device_id=(me, z + 1), device_id_type=MESH)

    for load in loads:
        load.start()

    for j in range(levels):
        ext_ref[:, j, :] = gates_ref[j]
    for j in range(levels, ext_ref.shape[1]):
        ext_ref[:, j, :] = jnp.broadcast_to(seg_ref[...].astype(F32), (heads, rows))

    pl.semaphore_wait(
        barrier, spread + not_first.astype(jnp.int32) + not_last.astype(jnp.int32)
    )

    slab = rows // PARTS

    def part_rows(part):
        return pl.ds(part * slab, slab)

    def own_right(part):
        return remote(
            og_hbm.at[part_rows(part)],
            gath.at[z, part_rows(part)],
            ag_right.at[z, part],
            ag_recv.at[z, part],
            (me, z + 1),
        )

    def own_left(part):
        return remote(
            og_hbm.at[part_rows(part)],
            gath.at[z, part_rows(part)],
            ag_left.at[z, part],
            ag_recv.at[z, part],
            (me, z - 1),
        )

    def pass_right(owner, part):
        block = gath.at[owner, part_rows(part)]
        return remote(
            block, block, ag_right.at[owner, part], ag_recv.at[owner, part], (me, z + 1)
        )

    def pass_left(owner, part):
        block = gath.at[owner, part_rows(part)]
        return remote(block, block, ag_left.at[owner, part], ag_recv.at[owner, part], (me, z - 1))

    for part in range(PARTS):

        @pl.when(not_last)
        def _():
            own_right(part).start()

        @pl.when(not_first)
        def _():
            own_left(part).start()

    def head_k(h):
        return pl.ds(pl.multiple_of(h * dk, dk), dk)

    def head_v(h):
        return pl.ds(pl.multiple_of(h * dv, dv), dv)

    loads[0].wait()
    loads[1].wait()

    @pl.loop(0, heads)
    def _(h):
        cols = ext_ref[h].T
        cols_ref[h] = cols
        seg = cols[:, levels : levels + 1]
        keep = (seg == seg[rows - 1 : rows, :]).astype(F32)
        masked = (k_ref[:, head_k(h)].astype(F32) * keep).astype(BF16)
        state_out[0, h] = mm(masked, v_ref[:, head_v(h)], 0, 0).astype(BF16)

    seg_row = ext_ref[0, levels : levels + 1, :]
    lane = dv
    first = jnp.broadcast_to(seg_row[:, 0:1], (1, lane))
    last = jnp.broadcast_to(seg_row[:, rows - 1 : rows], (1, lane))
    marks_out[0, 0:8, :] = jnp.broadcast_to(first, (8, lane))
    marks_out[0, 8:16, :] = jnp.broadcast_to(last, (8, lane))

    split = heads // 2 if heads % 2 == 0 else 0

    def own_half():
        return pl.ds(bits[0] * split, split)

    def hop(s):
        block = (s, own_half()) if s and split else s
        return (
            remote(
                state_out.at[block],
                state_in.at[block],
                st_send.at[s],
                st_recv.at[s],
                (partners[s], z),
            ),
            remote(
                marks_out.at[s], marks_in.at[s], mk_send.at[s], mk_recv.at[s], (partners[s], z)
            ),
        )

    def hop_share(s):
        block = state_in.at[s, own_half()]
        return remote(block, block, fs_send.at[s], fs_recv.at[s], (partners[0], z))

    def hop_start(s):
        for copy in hop(s):
            copy.start()

    def hop_finish(s):
        for copy in hop(s):
            copy.wait_recv()
        if s and split:
            hop_share(s).start()
            hop_share(s).wait_recv()
        up = bits[s].astype(F32)
        own_first, own_last = marks_out[s, 0:1, :], marks_out[s, 8:9, :]
        its_first, its_last = marks_in[s, 0:1, :], marks_in[s, 8:9, :]
        joined = (its_last == own_last).astype(F32)
        linked = (its_last == first).astype(F32) * up
        mine = up + (1 - up) * joined
        theirs = (1 - up) + up * joined
        last_section = s == spread - 1

        @pl.loop(0, heads)
        def _(h):
            partner = state_in[s, h].astype(F32)
            pieces[s, h] = (partner * linked).astype(BF16)
            if not last_section:
                state_out[s + 1, h] = (
                    state_out[s, h].astype(F32) * mine + partner * theirs
                ).astype(BF16)

        if not last_section:
            marks_out[s + 1, 0:8, :] = jnp.broadcast_to(
                up * its_first + (1 - up) * own_first, (8, lane)
            )
            marks_out[s + 1, 8:16, :] = jnp.broadcast_to(
                up * own_last + (1 - up) * its_last, (8, lane)
            )
            hop_start(s + 1)

    if spread:
        hop_start(0)

    table_ref[...] = table(
        cols_ref[0][:, levels : levels + 1], ext_ref[0, levels : levels + 1, :], rows, near
    )
    tile = 256
    middle = rows // 2
    loads[2].wait()

    def near_forward(low, high):
        @pl.loop(low, high)
        def _(h):
            cols = cols_ref[h]
            weights[h, 0:middle, middle:rows] = jnp.zeros((middle, rows - middle), BF16)
            probs[h, 0:middle, middle:rows] = jnp.zeros((middle, rows - middle), BF16)
            for low_row, high_row in ((0, middle), (middle, rows)):
                level = table_ref[low_row:high_row, 0:high_row]
                weight = jnp.zeros(level.shape, F32)
                for j in range(near):
                    weight = jnp.where(level == j, cols[low_row:high_row, j : j + 1], weight)
                weights[h, low_row:high_row, 0:high_row] = weight.astype(BF16)
                scores = mm(q_ref[low_row:high_row, head_k(h)], k_ref[0:high_row, head_k(h)], 1, 1)
                p = (weight * scores).astype(BF16)
                probs[h, low_row:high_row, 0:high_row] = p
                near_out[low_row:high_row, head_v(h)] = mm(p, v_ref[0:high_row, head_v(h)])

    done = 0
    for s in range(spread):
        upto = heads * (s + 1) // spread
        near_forward(done, upto)
        done = upto
        hop_finish(s)
    if done < heads:
        near_forward(done, heads)

    def far_gates(h):
        cols = cols_ref[h]
        seg = cols[:, levels : levels + 1]
        keep = (seg == seg[0:1, :]).astype(F32)
        return [cols[:, near + j : near + j + 1] * keep for j in range(far)]

    @pl.loop(0, heads)
    def _(h):
        gates = far_gates(h)
        q = q_ref[:, head_k(h)]
        out = near_out[:, head_v(h)]
        for j in range(far):
            out = out + gates[j] * mm(q, pieces[j, h])
        mixed_ref[:, head_v(h)] = out.astype(BF16)

    loads[3].wait()
    loads[4].wait()

    flip = (z < n_head - z).astype(jnp.int32)

    def project(at, at_rows):
        dest = flip * (n_head - 1 - at) + (1 - flip) * at

        @pl.loop(0, width // tile)
        def _(c):
            from_col = pl.multiple_of(dest * width + c * tile, tile)
            part = mm(mixed_ref[at_rows, :], w_ref[:, pl.ds(from_col, tile)])
            pj[dest, at_rows, pl.ds(pl.multiple_of(c * tile, tile), tile)] = part.astype(BF16)

    def product(block, owner, at_rows, fresh):
        @pl.loop(0, inner // tile)
        def _(r):
            at = pl.ds(pl.multiple_of(r * tile, tile), tile)
            term = mm(
                block[at_rows, :],
                w_ref[at, pl.ds(pl.multiple_of(owner * width, width), width)],
                1,
                1,
            )
            acc[at_rows, at] = term if fresh else acc[at_rows, at] + term

    def sum_right(dest, part, src=rsr):
        return remote(
            src.at[dest, part_rows(part)],
            rsr.at[dest, part_rows(part)],
            rs_right.at[dest, part],
            rs_recv_r.at[dest, part],
            (me, z + 1),
        )

    def sum_left(dest, part, src=rsl):
        return remote(
            src.at[dest, part_rows(part)],
            rsl.at[dest, part_rows(part)],
            rs_left.at[dest, part],
            rs_recv_l.at[dest, part],
            (me, z - 1),
        )

    def send_sum(buf, make, has_upstream, dest, part):
        @pl.when(has_upstream)
        def _():
            make(dest, part).wait_recv()

            @pl.loop(0, slab // 64)
            def _(r):
                at = pl.ds(pl.multiple_of(part * slab + r * 64, 64), 64)
                buf[dest, at, :] = (
                    buf[dest, at, :].astype(F32) + pj[dest, at, :].astype(F32)
                ).astype(BF16)

            make(dest, part).start()

        @pl.when(jnp.logical_not(has_upstream))
        def _():
            make(dest, part, pj).start()

    def sums(phase, part):
        reach = n_head - phase

        @pl.when(z + reach < n_head)
        def _():
            send_sum(rsr, sum_right, not_first, z + reach, part)

        @pl.when(z - reach >= 0)
        def _():
            send_sum(rsl, sum_left, not_last, z - reach, part)

    def forwards(phase, part):
        @pl.when(z - phase >= 0)
        def _():
            pass_right(z - phase, part).wait_recv()

            @pl.when(not_last)
            def _():
                pass_right(z - phase, part).start()

        @pl.when(z + phase < n_head)
        def _():
            pass_left(z + phase, part).wait_recv()

            @pl.when(not_first)
            def _():
                pass_left(z + phase, part).start()

    def products(phase, at_rows):
        @pl.when(z - phase >= 0)
        def _():
            product(gath.at[z - phase], z - phase, at_rows, False)

        @pl.when(z + phase < n_head)
        def _():
            product(gath.at[z + phase], z + phase, at_rows, False)

    def leaves(part):
        at = part_rows(part)

        @pl.loop(0, heads)
        def _(h):
            g = acc[at, head_v(h)].astype(BF16)
            cot[at, head_v(h)] = g
            g = g.astype(F32)
            q = q_ref[at, head_k(h)]
            gates = far_gates(h)
            for j in range(far):
                term = mm(q, (g * gates[j][part * slab : (part + 1) * slab]).astype(BF16), 0, 0)
                if part:
                    term = leaf_acc[j, h] + term
                if part < PARTS - 1:
                    leaf_acc[j, h] = term
                else:
                    dual_out[j, h] = term.astype(BF16)

    whole_block = pl.ds(0, rows)
    for part in range(PARTS):
        project(0, part_rows(part))
        if n_head > 1:
            sums(1, part)
    if n_head > 1:
        project(1, whole_block)
        for part in range(PARTS):
            forwards(1, part)
    for at in range(2, n_head):
        project(at, whole_block)
    product(og_ref, z, whole_block, True)
    if n_head > 1:
        products(1, whole_block)
    for phase in range(2, n_head):
        for part in range(PARTS):
            forwards(phase, part)
            sums(phase, part)
            products(phase, part_rows(part))
            if phase == n_head - 1:
                leaves(part)
    if n_head < 3:
        for part in range(PARTS):
            leaves(part)

    starts = [sum(spread - i for i in range(s)) for s in range(spread + 1)]

    def dual_hop(s):
        block = pl.ds(starts[s], spread - s)
        if s and split:
            block = (block, pl.ds(bits[0] * split, split))
        return remote(
            dual_out.at[block], dual_in.at[block], du_send.at[s], du_recv.at[s], (partners[s], z)
        )

    def dual_share(s):
        block = (pl.ds(starts[s], spread - s), pl.ds(bits[0] * split, split))
        return remote(
            dual_in.at[block], dual_in.at[block], ds_send.at[s], ds_recv.at[s], (partners[0], z)
        )

    def dual_finish(s):
        dual_hop(s).wait_recv()
        if s and split:
            dual_share(s).start()
            dual_share(s).wait_recv()
        up = bits[s].astype(F32)
        own_first, its_first = marks_out[s, 0:1, :], marks_in[s, 0:1, :]
        joined = (its_first == own_first).astype(F32)
        linked = (its_first == last).astype(F32) * (1 - up)
        mine = (1 - up) + up * joined
        theirs = up + (1 - up) * joined

        @pl.loop(0, heads)
        def _(h):
            gain = dual_in[starts[s], h].astype(F32) * linked
            inbound[h] = gain if s == 0 else inbound[h] + gain
            for j in range(1, spread - s):
                dual_out[starts[s + 1] + j - 1, h] = (
                    dual_out[starts[s] + j, h].astype(F32) * mine
                    + dual_in[starts[s] + j, h].astype(F32) * theirs
                ).astype(BF16)

        if s < spread - 1:
            dual_hop(s + 1).start()

    if spread:
        dual_hop(0).start()

    stores = [
        pltpu.make_async_copy(source, target, out_sem.at[i])
        for i, (source, target) in enumerate(((dq_ref, dq_hbm), (dk_ref, dk_hbm), (dv_ref, dv_hbm)))
    ]

    def near_backward(low, high):
        @pl.loop(low, high)
        def _(h):
            q, k = q_ref[:, head_k(h)], k_ref[:, head_k(h)]
            v, g = v_ref[:, head_v(h)], cot[:, head_v(h)]
            near_out[:, head_v(h)] = mm(probs[h], g, 0, 0)
            grads = (weights[h].astype(F32) * mm(g, v, 1, 1)).astype(BF16)
            acc[:, head_k(h)] = mm(grads, q, 0, 0)
            dq = mm(grads, k)
            gates = far_gates(h)
            for j in range(far):
                dq = dq + gates[j] * mm(g, pieces[j, h], 1, 1)
            dq_ref[:, head_k(h)] = dq.astype(BF16)

    done = 0
    for s in range(spread):
        upto = heads * (s + 1) // spread
        near_backward(done, upto)
        done = upto
        dual_finish(s)
    if done < heads:
        near_backward(done, heads)
    stores[0].start()

    @pl.loop(0, heads)
    def _(h):
        seg = cols_ref[h][:, levels : levels + 1]
        keep = (seg == seg[rows - 1 : rows, :]).astype(F32)
        near_dk, near_dv = acc[:, head_k(h)], near_out[:, head_v(h)]
        if spread:
            state = inbound[h].astype(BF16)
            near_dk = near_dk + keep * mm(v_ref[:, head_v(h)], state, 1, 1)
            near_dv = near_dv + keep * mm(k_ref[:, head_k(h)], state)
        dk_ref[:, head_k(h)] = near_dk.astype(BF16)
        dv_ref[:, head_v(h)] = near_dv.astype(BF16)

    stores[1].start()
    stores[2].start()

    def last_sum(part, upstream):
        @pl.loop(0, slab // 64)
        def _(r):
            at = pl.ds(pl.multiple_of(part * slab + r * 64, 64), 64)
            total = pj[z, at, :].astype(F32)
            for buf in upstream:
                total = total + buf[z, at, :].astype(F32)
            mixed_ref[at, :] = total.astype(BF16)

    def mixed_store(part):
        return pltpu.make_async_copy(
            mixed_ref.at[part_rows(part)], mixed_hbm.at[part_rows(part)], out_sem.at[3 + part]
        )

    for part in range(PARTS):

        @pl.when(not_first)
        def _():
            sum_right(z, part).wait_recv()

        @pl.when(not_last)
        def _():
            sum_left(z, part).wait_recv()

        @pl.when(not_first & not_last)
        def _():
            last_sum(part, (rsr, rsl))

        @pl.when(not_first & jnp.logical_not(not_last))
        def _():
            last_sum(part, (rsr,))

        @pl.when(not_last & jnp.logical_not(not_first))
        def _():
            last_sum(part, (rsl,))

        if n_head == 1:
            last_sum(part, ())
        mixed_store(part).start()

    for part in range(PARTS):

        @pl.when(not_last)
        def _():
            own_right(part).wait_send()

        @pl.when(not_first)
        def _():
            own_left(part).wait_send()

        for phase in range(1, n_head):
            reach = n_head - phase

            @pl.when((z - phase >= 0) & not_last)
            def _():
                pass_right(z - phase, part).wait_send()

            @pl.when((z + phase < n_head) & not_first)
            def _():
                pass_left(z + phase, part).wait_send()

            @pl.when(z + reach < n_head)
            def _():
                sum_right(z + reach, part).wait_send()

            @pl.when(z - reach >= 0)
            def _():
                sum_left(z - reach, part).wait_send()

    for s in range(spread):
        for copy in hop(s):
            copy.wait_send()
        dual_hop(s).wait_send()
        if s and split:
            dual_share(s).wait_send()
            hop_share(s).wait_send()
    for store in stores:
        store.wait()
    for part in range(PARTS):
        mixed_store(part).wait()


def shards(queries, keys, values, gates, segment_ids, out_weight, out_grad):
    rows = queries.shape[0]
    heads, levels = gates.shape[0], gates.shape[1]
    dk = queries.shape[1] // heads
    dv = values.shape[1] // heads
    near = (rows // SPAN).bit_length()
    n_ctx = lax.axis_size("ctx")
    n_head = lax.axis_size("head")
    spread = n_ctx.bit_length() - 1
    width = out_grad.shape[1]
    inner = out_weight.shape[0]
    size = -(-(levels + 1) // 8) * 8
    duals = max(spread * (spread + 1) // 2, 1)
    hops = max(spread, 1)
    dma = pltpu.SemaphoreType.DMA
    vmem = pl.BlockSpec(memory_space=pltpu.VMEM)
    hbm = pl.BlockSpec(memory_space=pl.ANY)
    return pl.pallas_call(
        functools.partial(kernel, n_ctx, n_head, heads, levels, near),
        in_specs=[hbm] * 5 + [vmem] * 2,
        out_specs=[hbm] * 4,
        out_shape=[
            jax.ShapeDtypeStruct((rows, width), BF16),
            jax.ShapeDtypeStruct(queries.shape, BF16),
            jax.ShapeDtypeStruct(keys.shape, BF16),
            jax.ShapeDtypeStruct(values.shape, BF16),
        ],
        scratch_shapes=[
            pltpu.VMEM(queries.shape, BF16),
            pltpu.VMEM(keys.shape, BF16),
            pltpu.VMEM(values.shape, BF16),
            pltpu.VMEM(out_grad.shape, BF16),
            pltpu.VMEM((rows, max(width, inner)), BF16),
            pltpu.VMEM(queries.shape, BF16),
            pltpu.VMEM(keys.shape, BF16),
            pltpu.VMEM(values.shape, BF16),
            pltpu.VMEM((heads, size, rows), F32),
            pltpu.VMEM((levels - near, heads, dk, dv), F32),
            pltpu.VMEM(out_weight.shape, BF16),
            pltpu.VMEM((n_head, rows, width), BF16),
            pltpu.VMEM((rows, inner), F32),
            pltpu.VMEM((rows, inner), F32),
            pltpu.VMEM((n_head, rows, width), BF16),
            pltpu.VMEM((n_head, rows, width), BF16),
            pltpu.VMEM((n_head, rows, width), BF16),
            pltpu.VMEM((heads, rows, rows), BF16),
            pltpu.VMEM((heads, rows, rows), BF16),
            pltpu.VMEM((rows, rows), jnp.int32),
            pltpu.VMEM((heads, rows, size), F32),
            pltpu.VMEM((rows, inner), BF16),
            pltpu.VMEM((hops, heads, dk, dv), BF16),
            pltpu.VMEM((hops, heads, dk, dv), BF16),
            pltpu.VMEM((hops, 16, dv), F32),
            pltpu.VMEM((hops, 16, dv), F32),
            pltpu.VMEM((hops, heads, dk, dv), BF16),
            pltpu.VMEM((duals, heads, dk, dv), BF16),
            pltpu.VMEM((duals, heads, dk, dv), BF16),
            pltpu.VMEM((heads, dk, dv), F32),
            dma((5,)),
            dma((3 + PARTS,)),
            dma((n_head, PARTS)),
            dma((n_head, PARTS)),
            dma((n_head, PARTS)),
            dma((n_head, PARTS)),
            dma((n_head, PARTS)),
            dma((n_head, PARTS)),
            dma((n_head, PARTS)),
            dma((hops,)),
            dma((hops,)),
            dma((hops,)),
            dma((hops,)),
            dma((hops,)),
            dma((hops,)),
            dma((hops,)),
            dma((hops,)),
            dma((hops,)),
            dma((hops,)),
        ],
        compiler_params=pltpu.CompilerParams(
            collective_id=0, has_side_effects=True, vmem_limit_bytes=60 << 20
        ),
        cost_estimate=pl.CostEstimate(
            flops=4 * rows * n_head * width * inner + 14 * rows * rows * dk * heads,
            bytes_accessed=40 << 20,
            transcendentals=0,
        ),
    )(
        queries,
        keys,
        values,
        out_grad,
        out_weight,
        gates.transpose(1, 0, 2),
        segment_ids.reshape(1, rows),
    )


def copy_kernel(*refs):
    count = (len(refs) - 2) // 3
    sources, targets, held = refs[:count], refs[count : 2 * count], refs[2 * count : 3 * count]
    into, out = refs[-2], refs[-1]
    pairs = []
    for i in range(count):
        slab = sources[i].shape[0] // 2
        for j in range(2):
            at = pl.ds(j * slab, slab)
            pairs.append(
                (
                    pltpu.make_async_copy(sources[i].at[at], held[i].at[at], into.at[2 * i + j]),
                    pltpu.make_async_copy(held[i].at[at], targets[i].at[at], out.at[2 * i + j]),
                )
            )
    for first, _ in pairs:
        first.start()
    for first, second in pairs:
        first.wait()
        second.start()
    for _, second in pairs:
        second.wait()


def results(arrays):
    spec = [pl.BlockSpec(memory_space=pl.ANY)] * len(arrays)
    return tuple(
        pl.pallas_call(
            copy_kernel,
            in_specs=spec,
            out_specs=spec,
            out_shape=[jax.ShapeDtypeStruct(a.shape, a.dtype) for a in arrays],
            scratch_shapes=[pltpu.VMEM(a.shape, a.dtype) for a in arrays]
            + [pltpu.SemaphoreType.DMA((2 * len(arrays),))] * 2,
            compiler_params=pltpu.CompilerParams(vmem_limit_bytes=60 << 20),
        )(*arrays)
    )


def solution(mesh):
    placed = (
        P("ctx", "head"),
        P("ctx", "head"),
        P("ctx", "head"),
        P("head", None, "ctx"),
        P("ctx"),
        P("head", None),
        P("ctx", "head"),
    )

    def body(*args):
        return results(shards(*args))

    return jax.shard_map(
        body,
        mesh=mesh,
        in_specs=placed,
        out_specs=(P("ctx", "head"), P("ctx", "head"), P("ctx", "head"), P("ctx", "head")),
        check_vma=False,
    )
```
